32 devices in a mesh: fsdp: 8 (over z, x), ctx: 2 (over y), tp: 2 (over core).
Axes of the slice: x: 2, y: 2, z: 4, core: 2. Of those that a mesh axis runs over, the one named last changes fastest.
Arguments:
- tokens: bfloat16 [8, 1024, 896], P('fsdp', 'ctx'), may hold values from -6 to 6
- positions: int32 [8, 1024], P('fsdp', 'ctx'), may hold values from 0 to 1021, as said below
- norm1_gain: bfloat16 [896], P('fsdp'), may hold values from 0.5 to 1.5
- q_weight: bfloat16 [896, 896], P('fsdp', 'tp'), may hold values from -0.1875 to 0.1875
- q_bias: bfloat16 [14, 64], P('tp', 'fsdp'), may hold values from -3 to 3
- key_projection: bfloat16 [896, 128], P('fsdp', 'tp'), may hold values from -0.1875 to 0.1875
- key_bias: bfloat16 [2, 64], P('tp', 'fsdp'), may hold values from -3 to 3
- value_projection: bfloat16 [896, 128], P('fsdp', 'tp'), may hold values from -0.1875 to 0.1875
- value_bias: bfloat16 [2, 64], P('tp', 'fsdp'), may hold values from -3 to 3
- o_weight: bfloat16 [896, 896], P('tp', 'fsdp'), may hold values from -1 to 1
- norm2_gain: bfloat16 [896], P('fsdp'), may hold values from 0.5 to 1.5
- gate_weight: bfloat16 [896, 4864], P('fsdp', 'tp'), may hold values from -0.1875 to 0.1875
- up_weight: bfloat16 [896, 4864], P('fsdp', 'tp'), may hold values from -0.1875 to 0.1875
- down_weight: bfloat16 [4864, 896], P('tp', 'fsdp'), may hold values from -0.25 to 0.25
- out_grad: bfloat16 [8, 1024, 896], P('fsdp', 'ctx'), may hold values from -6 to 6
Outputs:
- layer_out: bfloat16 [8, 1024, 896], P('fsdp', 'ctx')
- input_grad: float32 [8, 1024, 896], P('fsdp', 'ctx')
- norm1_gain_grad: float32 [896], P('fsdp')
- q_weight_grad: float32 [896, 896], P('fsdp', 'tp')
- q_bias_grad: float32 [14, 64], P('tp', 'fsdp')
- k_weight_grad: float32 [896, 128], P('fsdp', 'tp')
- k_bias_grad: float32 [2, 64], P('tp', 'fsdp')
- v_weight_grad: float32 [896, 128], P('fsdp', 'tp')
- v_bias_grad: float32 [2, 64], P('tp', 'fsdp')
- o_weight_grad: float32 [896, 896], P('tp', 'fsdp')
- norm2_gain_grad: float32 [896], P('fsdp')
- gate_weight_grad: float32 [896, 4864], P('fsdp', 'tp')
- up_weight_grad: float32 [896, 4864], P('fsdp', 'tp')
- down_weight_grad: float32 [4864, 896], P('tp', 'fsdp')
The draws below stay inside these ranges and needn't reach their ends.
Inputs may be any that keep to these rules, and one draw needn't show every extreme that they name: positions count 0, 1, 2, ... along each document and restart at 0 where a new document begins; every sequence begins with a 0.
All inputs are finite; a program needn't handle non-finite values.
Results may differ from the reference program's by a relative error of at most 0.039.
Values may be sent and summed in bfloat16 or wider, within the bound.
No kernel may reach another device: no remote copies, remote signals or barrier semaphores. Data moves between devices by JAX's collectives and lax.ppermute only.
A program may use at most 128 MiB of HBM per device.

```python
import jax
import jax.numpy as jnp
from jax import lax

MODEL_WIDTH = 896
QUERY_HEADS = 14
KEY_VALUE_HEADS = 2
HEAD_SIZE = 64
FF = 4864
SEQUENCE_TOKENS = 1024
ROWS = 512
SEQS = 8


def draw_positions(key, part):
    first_key, second_key, third_key = jax.random.split(jax.random.fold_in(key, 11), 3)
    head_length = jax.random.randint(first_key, (SEQS, 1), 1, ROWS // 2 + 1)
    tail_length = jax.random.randint(second_key, (SEQS, 1), 1, ROWS // 2 + 1)
    chosen_seq = jax.random.randint(third_key, (), 0, SEQS)
    is_chosen = (jnp.arange(SEQS, dtype=jnp.int32) == chosen_seq)[:, None]
    head_length = jnp.where(is_chosen, 1, head_length)
    tail_length = jnp.where(is_chosen, 1, tail_length)
    token_index = jnp.arange(SEQUENCE_TOKENS, dtype=jnp.int32)[None, :]
    tail_start = SEQUENCE_TOKENS - tail_length
    begin_at = jnp.where(token_index < head_length, 0, jnp.where(token_index < tail_start, head_length, tail_start))
    return (token_index - begin_at).astype(jnp.int32)


def block_levels(stream_key, dims, cuts, low, high):
    factor_of, own = 1.0, jax.random.fold_in(stream_key, 6)
    for position, parts in cuts:
        heights = jnp.exp(jax.random.uniform(jax.random.fold_in(own, position), (parts,), jnp.float32, low / len(cuts), high / len(cuts)))
        factor_of = factor_of * jnp.repeat(heights, dims[position] // parts).reshape([-1 if axis == position else 1 for axis in range(len(dims))])
    return factor_of


def gaussian(rng, shape, spread, most, cuts=(), held_as=jnp.bfloat16):
    drawn = spread * jax.random.normal(rng, shape, jnp.float32)
    if cuts:
        drawn = drawn * block_levels(rng, shape, cuts, -0.22, 0.18)
    return jnp.clip(drawn, -most, most).astype(held_as)


def setup_inputs(seed: int = 0) -> dict:
    seeds = jax.random.split(jax.random.key(seed), 16)
    tokens = gaussian(seeds[0], (SEQS, SEQUENCE_TOKENS, MODEL_WIDTH), 1.0, 6.0, ((0, 8), (1, 2)))
    positions = draw_positions(jax.random.fold_in(seeds[15], 71), 0)
    norm1_gain = jnp.clip(1.0 + 0.1 * jax.random.normal(seeds[2], (MODEL_WIDTH,), jnp.float32), 0.5, 1.5).astype(jnp.bfloat16)
    q_weight = gaussian(seeds[3], (MODEL_WIDTH, QUERY_HEADS * HEAD_SIZE), MODEL_WIDTH ** -0.5, 0.1875, ((0, 8), (1, 2)))
    q_bias = gaussian(seeds[4], (QUERY_HEADS, HEAD_SIZE), 0.5, 3.0, ((0, 2), (1, 8)))
    key_projection = gaussian(seeds[5], (MODEL_WIDTH, KEY_VALUE_HEADS * HEAD_SIZE), MODEL_WIDTH ** -0.5, 0.1875, ((0, 8), (1, 2)))
    key_bias = gaussian(seeds[6], (KEY_VALUE_HEADS, HEAD_SIZE), 0.5, 3.0, ((0, 2), (1, 8)))
    value_projection = gaussian(seeds[7], (MODEL_WIDTH, KEY_VALUE_HEADS * HEAD_SIZE), MODEL_WIDTH ** -0.5, 0.1875, ((0, 8), (1, 2)))
    value_bias = gaussian(seeds[8], (KEY_VALUE_HEADS, HEAD_SIZE), 0.5, 3.0, ((0, 2), (1, 8)))
    o_weight = gaussian(seeds[9], (QUERY_HEADS * HEAD_SIZE, MODEL_WIDTH), (QUERY_HEADS * HEAD_SIZE // 32) ** -0.5, 1.0, ((0, 2), (1, 8)))
    norm2_gain = jnp.clip(1.0 + 0.1 * jax.random.normal(seeds[10], (MODEL_WIDTH,), jnp.float32), 0.5, 1.5).astype(jnp.bfloat16)
    gate_weight = gaussian(seeds[11], (MODEL_WIDTH, FF), MODEL_WIDTH ** -0.5, 0.1875, ((0, 8), (1, 2)))
    up_weight = gaussian(seeds[12], (MODEL_WIDTH, FF), MODEL_WIDTH ** -0.5, 0.1875, ((0, 8), (1, 2)))
    down_weight = gaussian(seeds[13], (FF, MODEL_WIDTH), (FF // 8) ** -0.5, 0.25, ((0, 2), (1, 8)))
    out_grad = gaussian(seeds[14], (SEQS, SEQUENCE_TOKENS, MODEL_WIDTH), 1.0, 6.0, ((0, 8), (1, 2)))
    return dict(tokens=tokens, positions=positions, norm1_gain=norm1_gain, q_weight=q_weight, q_bias=q_bias, key_projection=key_projection, key_bias=key_bias, value_projection=value_projection, value_bias=value_bias, o_weight=o_weight, norm2_gain=norm2_gain, gate_weight=gate_weight, up_weight=up_weight, down_weight=down_weight, out_grad=out_grad)


NORM_EPS = 1e-06
MASK_FILL = -1e+30

@jax.custom_vjp
def lower_precision(v):
    return lax.optimization_barrier(v.astype(jnp.bfloat16)).astype(jnp.float32)

@jax.custom_vjp
def lower_precision_back(v):
    return v

def low_keep(v):
    return (lower_precision(v), None)

def low_pass(kept, grad):
    return (grad,)

def back_keep(v):
    return (v, None)

def back_low(kept, grad):
    return (lower_precision(grad),)
lower_precision.defvjp(low_keep, low_pass)
lower_precision_back.defvjp(back_keep, back_low)

def matrix_product_high(left, right):
    return jnp.dot(left, right, precision=lax.Precision.HIGHEST)

def rotary_apply(tensor, cosine_table, sine_table):
    half_dim = tensor.shape[-1] // 2
    turned = jnp.concatenate([-tensor[..., half_dim:], tensor[..., :half_dim]], axis=-1)
    return tensor * cosine_table + turned * sine_table

def rms_norm(source, gain_vec):
    inverse = lax.rsqrt(lax.optimization_barrier(jnp.mean(source * source, axis=-1, keepdims=True)) + NORM_EPS)
    return source * inverse * gain_vec

def forward(params, inputs, cosine_table, sine_table, token_index, doc_start):
    gain_one, w_query, b_query, w_key, b_key, value_weight_matrix, value_bias_vector, w_out, gain_two, w_gate, w_up, w_down = params
    query_group_size = QUERY_HEADS // KEY_VALUE_HEADS
    first_norm = lower_precision(rms_norm(inputs, gain_one))
    q_lin = lower_precision_back(matrix_product_high(first_norm, w_query) + b_query.reshape(-1))
    key_linear = lower_precision_back(matrix_product_high(first_norm, w_key) + b_key.reshape(-1))
    value_matrix = lower_precision(lower_precision_back(matrix_product_high(first_norm, value_weight_matrix) + value_bias_vector.reshape(-1))).reshape(SEQUENCE_TOKENS, KEY_VALUE_HEADS, HEAD_SIZE)
    query_matrix = lower_precision(rotary_apply(q_lin.reshape(SEQUENCE_TOKENS, QUERY_HEADS, HEAD_SIZE), cosine_table[:, None, :], sine_table[:, None, :]))
    key_row_block = lower_precision(rotary_apply(key_linear.reshape(SEQUENCE_TOKENS, KEY_VALUE_HEADS, HEAD_SIZE), cosine_table[:, None, :], sine_table[:, None, :]))
    score_scale = HEAD_SIZE ** (-0.5)
    rows_per_block = 512 if SEQUENCE_TOKENS % 512 == 0 else SEQUENCE_TOKENS
    block_list = SEQUENCE_TOKENS // rows_per_block

    def attend_block(seq_item):
        query_block, index_block, start_block = seq_item
        raw_scores = lower_precision_back(jnp.einsum('bkgd,skd->kgbs', query_block, key_row_block, precision=lax.Precision.HIGHEST))
        visible = (token_index[None, :] <= index_block[:, None]) & (token_index[None, :] >= start_block[:, None])
        scores = jnp.where(visible[None, None], raw_scores * score_scale, MASK_FILL)
        top_score = lax.optimization_barrier(jnp.max(scores, axis=-1, keepdims=True))
        weights = jnp.exp(scores - top_score)
        probabilities = weights / lax.optimization_barrier(jnp.sum(weights, axis=-1, keepdims=True))
        return jnp.einsum('kgbs,skd->bkgd', lower_precision(probabilities), value_matrix, precision=lax.Precision.HIGHEST)
    query_block_list = query_matrix.reshape(block_list, rows_per_block, KEY_VALUE_HEADS, query_group_size, HEAD_SIZE)
    attended = lax.map(jax.checkpoint(attend_block), (query_block_list, token_index.reshape(block_list, rows_per_block), doc_start.reshape(block_list, rows_per_block)))
    attn_low = lower_precision(lower_precision_back(attended.reshape(SEQUENCE_TOKENS, QUERY_HEADS * HEAD_SIZE)))
    middle = inputs + lower_precision_back(matrix_product_high(attn_low, w_out))
    norm_two = lower_precision(rms_norm(middle, gain_two))
    gate_proj = lower_precision_back(matrix_product_high(norm_two, w_gate))
    up_proj = lower_precision_back(matrix_product_high(norm_two, w_up))
    hidden = lower_precision(jax.nn.silu(gate_proj) * up_proj)
    return middle + lower_precision_back(matrix_product_high(hidden, w_down))

def reference(tokens, positions, norm1_gain, q_weight, q_bias, key_projection, key_bias, value_projection, value_bias, o_weight, norm2_gain, gate_weight, up_weight, down_weight, out_grad):
    params = tuple((weight.astype(jnp.float32) for weight in (norm1_gain, q_weight, q_bias, key_projection, key_bias, value_projection, value_bias, o_weight, norm2_gain, gate_weight, up_weight, down_weight)))
    token_index = jnp.arange(SEQUENCE_TOKENS, dtype=jnp.int32)
    inv_freq = 1000000.0 ** (-jnp.arange(0, HEAD_SIZE, 2, dtype=jnp.float32) / HEAD_SIZE)

    def one_sequence(running, seq_item):
        seq_tokens, seq_positions, seq_grad = seq_item
        angles = seq_positions.astype(jnp.float32)[:, None] * inv_freq[None, :]
        angles = jnp.concatenate([angles, angles], axis=-1)
        cosine_table = jnp.cos(angles)
        sine_table = jnp.sin(angles)
        doc_start = (token_index - seq_positions.astype(jnp.int32)).astype(jnp.int32)

        def run_layer(weights_now, inputs):
            return forward(weights_now, inputs, cosine_table, sine_table, token_index, doc_start)
        layer_value, pull_back = jax.vjp(run_layer, params, seq_tokens.astype(jnp.float32))
        param_grads, input_grad = pull_back(seq_grad.astype(jnp.float32))
        running = jax.tree.map(jnp.add, running, param_grads)
        return (running, (layer_value.astype(jnp.bfloat16), input_grad))
    start_grads = jax.tree.map(jnp.zeros_like, params)
    totals, outputs = lax.scan(one_sequence, start_grads, (tokens, positions, out_grad))
    layer_out, input_grad = outputs
    return (layer_out, input_grad, totals[0], totals[1], totals[2], totals[3], totals[4], totals[5], totals[6], totals[7], totals[8], totals[9], totals[10], totals[11])
```

```python
import jax
import jax.numpy as jnp
from jax import lax
from jax.sharding import PartitionSpec as P

NORM_EPS = 1e-06
MASK_FILL = -1e30
SMALL_ROWS = 16


def product(left, right):
    return jnp.dot(left, right, preferred_element_type=jnp.float32)


def inner_prod(left, right):
    return lax.dot_general(
        left, right, (((0,), (0,)), ((), ())), preferred_element_type=jnp.float32
    )


def times_trans(left, right):
    return lax.dot_general(
        left, right, (((1,), (1,)), ((), ())), preferred_element_type=jnp.float32
    )


def low(value):
    return value.astype(jnp.bfloat16)


def wide(value):
    return value.astype(jnp.float32)


def rotary_apply(tensor, cosine_table, sine_table):
    half_dim = tensor.shape[-1] // 2
    turned = jnp.concatenate([-tensor[..., half_dim:], tensor[..., :half_dim]], axis=-1)
    return tensor * cosine_table + turned * sine_table


def unrotate(upstream, cosine_table, sine_table):
    half_dim = upstream.shape[-1] // 2
    shifted = upstream * sine_table
    turned_back = jnp.concatenate([shifted[..., half_dim:], -shifted[..., :half_dim]], axis=-1)
    return upstream * cosine_table + turned_back


def norm_back(upstream, source, inverse, gain_vec):
    scaled = upstream * gain_vec
    gain_grad = jnp.sum(upstream * source * inverse, axis=0)
    input_part = inverse * scaled - source * inverse**3 * jnp.mean(
        scaled * source, axis=-1, keepdims=True
    )
    return (input_part, gain_grad)


def fsdp_place():
    index = lax.axis_index("fsdp")
    return index // 2, index % 2


def gather_pieces(shard):
    count = lax.axis_size("fsdp")
    depth = count // 2
    below, above = [shard], [shard]
    below_x = [lax.ppermute(shard, "fsdp", [(i, i ^ 1) for i in range(count)])]
    above_x = [below_x[0]]
    for step in range(1, depth):
        below.append(
            lax.ppermute(
                below[-1], "fsdp", [(i, i + 2) for i in range(count - 2) if i // 2 >= step - 1]
            )
        )
        above.append(
            lax.ppermute(
                above[-1],
                "fsdp",
                [(i, i - 2) for i in range(2, count) if i // 2 + step - 1 < depth],
            )
        )
        below_x.append(
            lax.ppermute(
                below[-1], "fsdp", [(i, i ^ 1) for i in range(count) if i // 2 >= step]
            )
        )
        above_x.append(
            lax.ppermute(
                above[-1], "fsdp", [(i, i ^ 1) for i in range(count) if i // 2 + step < depth]
            )
        )
    return below, above, below_x, above_x


def assemble(pieces, first, rows):
    count = lax.axis_size("fsdp")
    depth = count // 2
    z, x = fsdp_place()
    below, above, below_x, above_x = pieces
    cols = below[0].shape[1]
    full = jnp.zeros((count * rows, cols), below[0].dtype)

    def cut(value):
        return value[first : first + rows]

    for distance in range(depth):
        at = lax.rem(z + distance, depth)
        for up_list, down_list, side in ((above, below, x), (above_x, below_x, 1 - x)):
            if distance == 0:
                piece = cut(up_list[0])
            else:
                piece = jnp.where(
                    z + distance < depth, cut(up_list[distance]), cut(down_list[depth - distance])
                )
            full = lax.dynamic_update_slice(full, piece, ((2 * at + side) * rows, 0))
    return full


def scatter_sum(full):
    count = lax.axis_size("fsdp")
    depth = count // 2
    z, x = fsdp_place()

    def block(target, side):
        return lax.dynamic_index_in_dim(full, 2 * target + side, 0, keepdims=False)

    def pair_sum(target, pairs):
        return wide(block(target, x)) + wide(lax.ppermute(block(target, 1 - x), "fsdp", pairs))

    up = down = None
    for distance in range(depth - 1, 0, -1):
        valid_up = [i for i in range(count) if i // 2 + distance < depth]
        valid_down = [i for i in range(count) if i // 2 >= distance]
        sum_up = pair_sum(jnp.minimum(z + distance, depth - 1), [(i, i ^ 1) for i in valid_up])
        sum_down = pair_sum(jnp.maximum(z - distance, 0), [(i, i ^ 1) for i in valid_down])
        if up is not None:
            sum_up = sum_up + wide(up)
            sum_down = sum_down + wide(down)
        up = lax.ppermute(low(sum_up), "fsdp", [(i, i + 2) for i in valid_up])
        down = lax.ppermute(low(sum_down), "fsdp", [(i, i - 2) for i in valid_down])
    total = pair_sum(z, [(i, i ^ 1) for i in range(count)])
    if up is not None:
        total = total + wide(up) + wide(down)
    return total


def swap_cores(value):
    count = lax.axis_size("tp")
    return lax.ppermute(value, "tp", [(i, (i + 1) % count) for i in range(count)])


def from_ctx(value, ahead):
    count = lax.axis_size("ctx")
    return lax.ppermute(value, "ctx", [((i + ahead) % count, i) for i in range(count)])


def to_ctx(value, ahead):
    count = lax.axis_size("ctx")
    return lax.ppermute(value, "ctx", [(i, (i + ahead) % count) for i in range(count)])


def half_rows(value, which):
    rows = value.shape[0] // 2
    return lax.dynamic_slice_in_dim(value, which * rows, rows, 0)


def join_halves(mine, others, core):
    return jnp.concatenate(
        [jnp.where(core == 0, mine, others), jnp.where(core == 0, others, mine)], axis=0
    )


def ctx_blocks(value, core):
    blocks = []
    mine = half_rows(value, core)
    for ahead in range(1, lax.axis_size("ctx")):
        got = from_ctx(mine, ahead)
        blocks.append(join_halves(got, swap_cores(got), core))
    return blocks


def core_sum(value, core):
    return low(wide(half_rows(value, core)) + wide(swap_cores(half_rows(value, 1 - core))))


def block_sums(own, others, core):
    sent = [to_ctx(core_sum(other, core), ahead + 1) for ahead, other in enumerate(others)]
    total = wide(core_sum(own, core))
    for part in sent:
        total = total + wide(part)
    total = low(total)
    return join_halves(total, swap_cores(total), core)


def pick(choices, index):
    out = choices[0]
    for number, choice in enumerate(choices[1:], 1):
        out = jnp.where(index == number, choice, out)
    return out


def body(
    tokens,
    positions,
    norm1_gain,
    q_weight,
    q_bias,
    key_projection,
    key_bias,
    value_projection,
    value_bias,
    o_weight,
    norm2_gain,
    gate_weight,
    up_weight,
    down_weight,
    out_grad,
):
    row_count, width = tokens.shape[1:]
    shards = lax.axis_size("fsdp")
    ctx_count = lax.axis_size("ctx")
    ctx = lax.axis_index("ctx")
    core = lax.axis_index("tp")
    head_dim = key_projection.shape[1]
    head_count = q_weight.shape[1] // head_dim
    q_cols = head_count * head_dim
    query_rows = row_count * head_count
    score_scale = head_dim ** (-0.5)
    shard_rows = q_weight.shape[0]
    hidden_cols = gate_weight.shape[1] // ctx_count
    bias_cols = q_bias.shape[1]

    small = jnp.concatenate(
        [norm1_gain, norm2_gain, q_bias.reshape(-1), key_bias.reshape(-1), value_bias.reshape(-1)]
    )
    qkv_shard = jnp.concatenate([q_weight, key_projection, value_projection], axis=1)
    qkv_cols = qkv_shard.shape[1]
    small_row = jnp.pad(small[None, :], ((0, SMALL_ROWS - 1), (0, qkv_cols - small.shape[0])))
    attn_shard = jnp.concatenate([qkv_shard, small_row], axis=0)
    attn_pieces = gather_pieces(attn_shard)
    w_qkv = assemble(attn_pieces, 0, shard_rows)
    small_full = assemble(attn_pieces, shard_rows, SMALL_ROWS).reshape(
        shards, SMALL_ROWS, qkv_cols
    )[:, 0]
    gain_one = small_full[:, :shard_rows].reshape(-1)
    gain_two = small_full[:, shard_rows : 2 * shard_rows].reshape(-1)
    at = 2 * shard_rows
    b_query = (
        small_full[:, at : at + head_count * bias_cols]
        .reshape(shards, head_count, bias_cols)
        .transpose(1, 0, 2)
        .reshape(-1)
    )
    at += head_count * bias_cols
    b_key = small_full[:, at : at + bias_cols].reshape(-1)
    b_value = small_full[:, at + bias_cols : at + 2 * bias_cols].reshape(-1)
    b_qkv = jnp.concatenate([b_query, b_key, b_value])

    o_trans = assemble(gather_pieces(o_weight.T), 0, shard_rows)

    def my_columns(weight):
        return pick(
            [weight[:, i * hidden_cols : (i + 1) * hidden_cols] for i in range(ctx_count)], ctx
        )

    w_gate = assemble(gather_pieces(my_columns(gate_weight)), 0, shard_rows)
    w_up = assemble(gather_pieces(my_columns(up_weight)), 0, shard_rows)
    down_trans = assemble(gather_pieces(my_columns(down_weight.T)), 0, shard_rows)

    grad_low = out_grad[0]
    grad_others = ctx_blocks(grad_low, core)

    first_row = ctx * row_count
    inputs = wide(tokens[0])
    seq_positions = positions[0]
    token_index = first_row + jnp.arange(row_count, dtype=jnp.int32)
    doc_start = token_index - seq_positions
    query_index = jnp.repeat(token_index, head_count)
    query_begin = jnp.repeat(doc_start, head_count)
    key_index = jnp.concatenate(
        [
            lax.rem(ctx + ahead, ctx_count) * row_count + jnp.arange(row_count, dtype=jnp.int32)
            for ahead in range(ctx_count)
        ]
    )
    inv_freq = 1000000.0 ** (-jnp.arange(0, head_dim, 2, dtype=jnp.float32) / head_dim)
    angles = wide(seq_positions)[:, None] * inv_freq[None, :]
    angles = jnp.concatenate([angles, angles], axis=-1)
    cosine_table = jnp.cos(angles)
    sine_table = jnp.sin(angles)
    inv_one = lax.rsqrt(jnp.mean(inputs * inputs, axis=-1, keepdims=True) + NORM_EPS)
    first_norm = low(inputs * inv_one * wide(gain_one))
    qkv_lin = product(first_norm, w_qkv) + wide(b_qkv)
    value_matrix = low(qkv_lin[:, q_cols + head_dim :])
    key_rows = low(rotary_apply(qkv_lin[:, q_cols : q_cols + head_dim], cosine_table, sine_table))
    key_value = jnp.concatenate([key_rows, value_matrix], axis=1)
    kv_all = jnp.concatenate(
        [key_value] + [from_ctx(key_value, ahead) for ahead in range(1, ctx_count)], axis=0
    )
    query_matrix = low(
        rotary_apply(
            qkv_lin[:, :q_cols].reshape(row_count, head_count, head_dim),
            cosine_table[:, None, :],
            sine_table[:, None, :],
        )
    ).reshape(query_rows, head_dim)
    key_part = kv_all[:, :head_dim]
    value_part = kv_all[:, head_dim:]
    visible = (key_index[None, :] <= query_index[:, None]) & (
        key_index[None, :] >= query_begin[:, None]
    )
    scores = times_trans(query_matrix, key_part) * score_scale
    top_score = jnp.max(jnp.where(visible, scores, MASK_FILL), axis=1)
    weights = jnp.where(visible, jnp.exp(scores - top_score[:, None]), 0.0)
    weight_sum = jnp.sum(weights, axis=1)
    partial_value = product(low(weights), value_part)
    log_total = top_score + jnp.log(weight_sum)
    attn_full = partial_value / weight_sum[:, None]
    attn_low = low(attn_full).reshape(row_count, q_cols)
    out_part = low(times_trans(attn_low, o_trans))
    middle = inputs + (wide(out_part) + wide(swap_cores(out_part)))
    inv_two = lax.rsqrt(jnp.mean(middle * middle, axis=-1, keepdims=True) + NORM_EPS)
    norm_two = low(middle * inv_two * wide(gain_two))
    norm_blocks = [norm_two] + ctx_blocks(norm_two, core)
    grad_blocks = [grad_low] + grad_others

    hidden_blocks, gate_grads, up_grads, norm_parts, down_parts = [], [], [], [], []
    for norm_block, grad_block in zip(norm_blocks, grad_blocks):
        hidden_grad = product(grad_block, down_trans)
        gate_proj = product(norm_block, w_gate)
        up_proj = product(norm_block, w_up)
        sigmoid_gate = jax.nn.sigmoid(gate_proj)
        silu_gate = gate_proj * sigmoid_gate
        hidden_blocks.append(low(silu_gate * up_proj))
        gate_grads.append(
            low(hidden_grad * up_proj * sigmoid_gate * (1.0 + gate_proj * (1.0 - sigmoid_gate)))
        )
        up_grads.append(low(hidden_grad * silu_gate))
        norm_parts.append(
            low(times_trans(gate_grads[-1], w_gate) + times_trans(up_grads[-1], w_up))
        )
        down_parts.append(low(times_trans(hidden_blocks[-1], down_trans)))
    norm_two_grad = wide(block_sums(norm_parts[0], norm_parts[1:], core))
    layer_out = low(middle + wide(block_sums(down_parts[0], down_parts[1:], core)))
    norm_all = jnp.concatenate(norm_blocks, axis=0)
    grad_all = jnp.concatenate(grad_blocks, axis=0)

    def ff_share(weight_grad):
        share = scatter_sum(low(weight_grad).reshape(shards, shard_rows, hidden_cols))
        low_share = low(share)
        parts = [low_share] + [from_ctx(low_share, ahead) for ahead in range(1, ctx_count)]
        return jnp.concatenate(
            [wide(pick(parts, lax.rem(i - ctx + ctx_count, ctx_count))) for i in range(ctx_count)],
            axis=1,
        )

    gate_share = ff_share(inner_prod(norm_all, jnp.concatenate(gate_grads, axis=0)))
    up_share = ff_share(inner_prod(norm_all, jnp.concatenate(up_grads, axis=0)))
    down_share = ff_share(inner_prod(grad_all, jnp.concatenate(hidden_blocks, axis=0))).T

    grad_top = wide(grad_low)
    middle_part, gain_two_grad = norm_back(norm_two_grad, middle, inv_two, wide(gain_two))
    middle_grad = grad_top + middle_part
    middle_low = low(middle_grad)
    attn_grad = low(product(middle_low, o_trans)).reshape(query_rows, head_dim)
    row_delta = jnp.sum(wide(attn_grad) * attn_full, axis=1)
    probabilities = jnp.where(visible, jnp.exp(scores - log_total[:, None]), 0.0)
    prob_grad = times_trans(attn_grad, value_part)
    score_grad = low(probabilities * (prob_grad - row_delta[:, None]) * score_scale)
    key_part_grad = inner_prod(score_grad, query_matrix)
    value_part_grad = inner_prod(low(probabilities), attn_grad)
    pair_grad = low(jnp.concatenate([key_part_grad, value_part_grad], axis=1))
    pair_mine = wide(pair_grad[:row_count])
    for ahead in range(1, ctx_count):
        pair_mine = pair_mine + wide(
            to_ctx(pair_grad[ahead * row_count : (ahead + 1) * row_count], ahead)
        )
    query_acc = product(score_grad, key_part)
    key_grad = low(unrotate(pair_mine[:, :head_dim], cosine_table, sine_table))
    value_grad = low(pair_mine[:, head_dim:])
    query_grad = low(
        unrotate(
            query_acc.reshape(row_count, head_count, head_dim),
            cosine_table[:, None, :],
            sine_table[:, None, :],
        )
    ).reshape(row_count, q_cols)
    qkv_grad = jnp.concatenate([query_grad, key_grad, value_grad], axis=1)
    bias_grad = low(jnp.sum(wide(qkv_grad), axis=0))
    qkv_w_grad = inner_prod(first_norm, qkv_grad)
    norm_one_part = low(times_trans(qkv_grad, w_qkv))
    norm_one_grad = wide(norm_one_part) + wide(swap_cores(norm_one_part))
    input_part, gain_one_grad = norm_back(norm_one_grad, inputs, inv_one, wide(gain_one))
    input_grad = middle_grad + input_part

    small_grad = jnp.concatenate(
        [
            low(gain_one_grad).reshape(shards, shard_rows),
            low(gain_two_grad).reshape(shards, shard_rows),
            bias_grad[:q_cols]
            .reshape(head_count, shards, bias_cols)
            .transpose(1, 0, 2)
            .reshape(shards, head_count * bias_cols),
            bias_grad[q_cols : q_cols + head_dim].reshape(shards, bias_cols),
            bias_grad[q_cols + head_dim :].reshape(shards, bias_cols),
        ],
        axis=1,
    )
    small_grad = jnp.pad(
        small_grad[:, None, :],
        ((0, 0), (0, SMALL_ROWS - 1), (0, qkv_cols - small_grad.shape[1])),
    )

    def ctx_sum(value):
        value = low(value)
        total = wide(value)
        for ahead in range(1, ctx_count):
            total = total + wide(from_ctx(value, ahead))
        return total

    o_share = ctx_sum(
        scatter_sum(low(inner_prod(middle_low, attn_low)).reshape(shards, shard_rows, q_cols))
    ).T
    attn_share = ctx_sum(
        scatter_sum(
            jnp.concatenate(
                [low(qkv_w_grad).reshape(shards, shard_rows, qkv_cols), small_grad], axis=1
            )
        )
    )
    small_share = attn_share[shard_rows]
    at = 2 * shard_rows
    q_bias_end = at + head_count * bias_cols
    return (
        layer_out[None],
        input_grad[None],
        small_share[:shard_rows],
        attn_share[:shard_rows, :q_cols],
        small_share[at:q_bias_end].reshape(head_count, bias_cols),
        attn_share[:shard_rows, q_cols : q_cols + head_dim],
        small_share[q_bias_end : q_bias_end + bias_cols][None],
        attn_share[:shard_rows, q_cols + head_dim :],
        small_share[q_bias_end + bias_cols : q_bias_end + 2 * bias_cols][None],
        o_share,
        small_share[shard_rows : 2 * shard_rows],
        gate_share,
        up_share,
        down_share,
    )


def solution(mesh):
    placed = (
        P("fsdp", "ctx", None),
        P("fsdp", "ctx"),
        P("fsdp"),
        P("fsdp", "tp"),
        P("tp", "fsdp"),
        P("fsdp", "tp"),
        P("tp", "fsdp"),
        P("fsdp", "tp"),
        P("tp", "fsdp"),
        P("tp", "fsdp"),
        P("fsdp"),
        P("fsdp", "tp"),
        P("fsdp", "tp"),
        P("tp", "fsdp"),
        P("fsdp", "ctx", None),
    )
    return jax.shard_map(
        body,
        mesh=mesh,
        in_specs=placed,
        out_specs=(
            P("fsdp", "ctx", None),
            P("fsdp", "ctx", None),
            P("fsdp"),
            P("fsdp", "tp"),
            P("tp", "fsdp"),
            P("fsdp", "tp"),
            P("tp", "fsdp"),
            P("fsdp", "tp"),
            P("tp", "fsdp"),
            P("tp", "fsdp"),
            P("fsdp"),
            P("fsdp", "tp"),
            P("fsdp", "tp"),
            P("tp", "fsdp"),
        ),
        check_vma=False,
    )
```

```python
import functools

import jax
import jax.numpy as jnp
from jax import lax
from jax.experimental import pallas as pl
from jax.experimental.pallas import tpu as pltpu
from jax.sharding import PartitionSpec as P

NORM_EPS = 1e-06
MASK_FILL = -1e30
SMALL_ROWS = 16
VMEM_BYTES = 48 * 1024 * 1024


def product(left, right):
    return jnp.dot(left, right, preferred_element_type=jnp.float32)


def inner_prod(left, right):
    return lax.dot_general(
        left, right, (((0,), (0,)), ((), ())), preferred_element_type=jnp.float32
    )


def times_trans(left, right):
    return lax.dot_general(
        left, right, (((1,), (1,)), ((), ())), preferred_element_type=jnp.float32
    )


def low(value):
    return value.astype(jnp.bfloat16)


def wide(value):
    return value.astype(jnp.float32)


def turn_halves(stack):
    half = stack.shape[1] // 2
    return jnp.concatenate([-stack[:, half:], stack[:, :half]], axis=1)


def unrotate(upstream, cosine, sine):
    half = upstream.shape[0] // 2
    shifted = upstream * sine
    turned_back = jnp.concatenate([shifted[half:], -shifted[:half]], axis=0)
    return upstream * cosine + turned_back


def fill_bias(base_ref, token_ref, bias_ref, blocks, rows, columns, span):
    token = token_ref[0:1, columns]
    begin = token_ref[1:2, columns]
    for number in range(blocks):
        size = min(rows, span - number * rows)
        index = base_ref[number] + lax.broadcasted_iota(jnp.int32, (size, token.shape[1]), 0)
        bias_ref[number * rows : number * rows + size, :] = jnp.where(
            (index <= token) & (index >= begin), 0.0, MASK_FILL
        )


def attend_kernel(heads, size, blocks, base_ref, token_ref, q_ref, k_ref, v_ref, attn_ref, low_ref, log_ref, bias_ref):
    rows = q_ref.shape[1]
    tile = bias_ref.shape[1]
    for start in range(0, rows, tile):
        columns = slice(start, start + tile)
        span = (blocks - 1) * rows + start + tile
        fill_bias(base_ref, token_ref, bias_ref, blocks, rows, columns, span)
        for head in range(heads):
            at = slice(head * size, (head + 1) * size)
            scores = product(k_ref[:span, :], q_ref[at, columns]) + bias_ref[:span, :]
            top = jnp.max(scores, axis=0, keepdims=True)
            weights = jnp.exp(scores - top)
            total = jnp.sum(weights, axis=0, keepdims=True)
            attn = product(v_ref[:, :span], low(weights)) / total
            attn_ref[at, columns] = attn
            low_ref[at, columns] = low(attn)
            log_ref[head : head + 1, columns] = top + jnp.log(total)


def attend_back_kernel(
    heads, size, blocks, scale, base_ref, token_ref, q_ref, k_ref, v_ref, kt_ref, grad_ref, attn_ref, log_ref,
    cosine_ref, sine_ref, query_grad_ref, pair_ref, bias_ref, dk_ref, dv_ref,
):
    rows = q_ref.shape[1]
    tile = bias_ref.shape[1]
    dk_ref[...] = jnp.zeros_like(dk_ref)
    dv_ref[...] = jnp.zeros_like(dv_ref)
    for start in range(0, rows, tile):
        columns = slice(start, start + tile)
        span = (blocks - 1) * rows + start + tile
        fill_bias(base_ref, token_ref, bias_ref, blocks, rows, columns, span)
        for head in range(heads):
            at = slice(head * size, (head + 1) * size)
            query = q_ref[at, columns]
            grad = grad_ref[at, columns]
            scores = product(k_ref[:span, :], query) + bias_ref[:span, :]
            probs = jnp.exp(scores - log_ref[head : head + 1, columns])
            delta = jnp.sum(wide(grad) * attn_ref[at, columns], axis=0, keepdims=True)
            score_grad = low(probs * (product(v_ref[:span, :], grad) - delta))
            dk_ref[:span, :] += times_trans(score_grad, query)
            dv_ref[:span, :] += times_trans(low(probs), grad)
            query_grad = product(kt_ref[:, :span], score_grad) * scale
            query_grad_ref[at, columns] = low(
                unrotate(query_grad, cosine_ref[:, columns], sine_ref[:, columns])
            )
    pair_ref[:size, :] = low(dk_ref[...].T)
    pair_ref[size:, :] = low(dv_ref[...].T)


def kernel_params():
    return pltpu.CompilerParams(vmem_limit_bytes=VMEM_BYTES)


def in_vmem(count):
    return [pl.BlockSpec(memory_space=pltpu.VMEM)] * count


def attend(bases, token_rows, queries, keys, values_t, heads):
    width, rows = queries.shape
    tile = min(256, rows)
    return pl.pallas_call(
        functools.partial(attend_kernel, heads, width // heads, bases.shape[0]),
        out_shape=(
            jax.ShapeDtypeStruct((width, rows), jnp.float32),
            jax.ShapeDtypeStruct((width, rows), jnp.bfloat16),
            jax.ShapeDtypeStruct((heads, rows), jnp.float32),
        ),
        in_specs=[pl.BlockSpec(memory_space=pltpu.SMEM)] + in_vmem(4),
        out_specs=tuple(in_vmem(3)),
        scratch_shapes=[pltpu.VMEM((keys.shape[0], tile), jnp.float32)],
        compiler_params=kernel_params(),
    )(bases, token_rows, queries, keys, values_t)


def attend_back(bases, token_rows, queries, keys, values, keys_t, grads, attn, logs, cosine, sine, heads, scale):
    width, rows = queries.shape
    size = width // heads
    total = keys.shape[0]
    tile = min(256, rows)
    return pl.pallas_call(
        functools.partial(attend_back_kernel, heads, size, bases.shape[0], scale),
        out_shape=(
            jax.ShapeDtypeStruct((width, rows), jnp.bfloat16),
            jax.ShapeDtypeStruct((2 * size, total), jnp.bfloat16),
        ),
        in_specs=[pl.BlockSpec(memory_space=pltpu.SMEM)] + in_vmem(10),
        out_specs=tuple(in_vmem(2)),
        scratch_shapes=[
            pltpu.VMEM((total, tile), jnp.float32),
            pltpu.VMEM((total, size), jnp.float32),
            pltpu.VMEM((total, size), jnp.float32),
        ],
        compiler_params=kernel_params(),
    )(bases, token_rows, queries, keys, values, keys_t, grads, attn, logs, cosine, sine)


def weight_grad_kernel(right_trans, shards, bit_ref, left_ref, right_ref, *refs):
    extra_ref, kept_ref, sent_ref = refs if len(refs) == 3 else (None, *refs)
    multiply = times_trans if right_trans else product
    full = multiply(left_ref[...], right_ref[...])
    rows = full.shape[0] // shards
    bit = bit_ref[0]
    for shard in range(shards):
        block = full[shard * rows : (shard + 1) * rows]
        if extra_ref is not None:
            block = jnp.concatenate([block, wide(extra_ref[shard])], axis=0)
        block = low(block)

        @pl.when(bit == shard % 2)
        def _(block=block, shard=shard):
            kept_ref[shard // 2] = block

        @pl.when(bit != shard % 2)
        def _(block=block, shard=shard):
            sent_ref[shard // 2] = block


def weight_grad(bit, left, right, right_trans, shards, extra=None):
    cols = right.shape[0] if right_trans else right.shape[1]
    rows = left.shape[0] // shards + (0 if extra is None else extra.shape[1])
    half = jax.ShapeDtypeStruct((shards // 2, rows, cols), jnp.bfloat16)
    operands = (left, right) if extra is None else (left, right, extra)
    return pl.pallas_call(
        functools.partial(weight_grad_kernel, right_trans, shards),
        out_shape=(half, half),
        in_specs=[pl.BlockSpec(memory_space=pltpu.SMEM)] + in_vmem(len(operands)),
        out_specs=tuple(in_vmem(2)),
        compiler_params=kernel_params(),
    )(bit, *operands)


def norm_back(upstream, source, inverse, gain_vec):
    scaled = upstream * gain_vec
    gain_grad = jnp.sum(upstream * source * inverse, axis=0)
    input_part = inverse * scaled - source * inverse**3 * jnp.mean(
        scaled * source, axis=-1, keepdims=True
    )
    return (input_part, gain_grad)


def index_bits():
    return (lax.axis_size("fsdp") - 1).bit_length()


def flip(value, bit):
    count = lax.axis_size("fsdp")
    return lax.ppermute(value, "fsdp", [(i, i ^ (1 << bit)) for i in range(count)])


def own_bit(bit):
    return lax.rem(lax.axis_index("fsdp") // (1 << bit), 2)


def gather_fsdp(shard):
    rows, cols = shard.shape
    full = shard[None]
    for bit in range(index_bits() - 1, -1, -1):
        other = flip(full, bit)
        upper = own_bit(bit) == 1
        full = jnp.stack(
            [jnp.where(upper, other, full), jnp.where(upper, full, other)], axis=1
        ).reshape(-1, rows, cols)
    return full


def scatter_sum(kept, sent):
    rows, cols = kept.shape[1:]
    parts = [kept, flip(sent, 0)]
    for bit in range(1, index_bits()):
        mine = own_bit(bit)

        def cut(which):
            halves = [
                lax.dynamic_index_in_dim(part.reshape(-1, 2, rows, cols), which, 1, keepdims=False)
                for part in parts
            ]
            return low(sum(wide(half) for half in halves))

        received = flip(cut(1 - mine), bit)
        parts = [cut(mine), received]
    return (wide(parts[0]) + wide(parts[1])).reshape(rows, cols)


def swap_cores(value):
    count = lax.axis_size("tp")
    return lax.ppermute(value, "tp", [(i, (i + 1) % count) for i in range(count)])


def from_ctx(value, ahead):
    count = lax.axis_size("ctx")
    return lax.ppermute(value, "ctx", [((i + ahead) % count, i) for i in range(count)])


def to_ctx(value, ahead):
    count = lax.axis_size("ctx")
    return lax.ppermute(value, "ctx", [(i, (i + ahead) % count) for i in range(count)])


def ctx_blocks(value):
    return [from_ctx(value, ahead) for ahead in range(1, lax.axis_size("ctx"))]


def block_sums(own, others):
    total = wide(own)
    for ahead, other in enumerate(others):
        total = total + wide(to_ctx(other, ahead + 1))
    total = low(total)
    return low(wide(total) + wide(swap_cores(total)))


def pick(choices, index):
    out = choices[0]
    for number, choice in enumerate(choices[1:], 1):
        out = jnp.where(index == number, choice, out)
    return out


def body(
    tokens,
    positions,
    norm1_gain,
    q_weight,
    q_bias,
    key_projection,
    key_bias,
    value_projection,
    value_bias,
    o_weight,
    norm2_gain,
    gate_weight,
    up_weight,
    down_weight,
    out_grad,
):
    row_count, width = tokens.shape[1:]
    shards = lax.axis_size("fsdp")
    ctx_count = lax.axis_size("ctx")
    ctx = lax.axis_index("ctx")
    head_dim = key_projection.shape[1]
    head_count = q_weight.shape[1] // head_dim
    q_cols = head_count * head_dim
    score_scale = head_dim ** (-0.5)
    shard_rows = q_weight.shape[0]
    own_x = own_bit(0).reshape(1)
    hidden_cols = gate_weight.shape[1] // ctx_count
    bias_cols = q_bias.shape[1]

    small = jnp.concatenate(
        [norm1_gain, norm2_gain, q_bias.reshape(-1), key_bias.reshape(-1), value_bias.reshape(-1)]
    )
    qkv_shard = jnp.concatenate([q_weight, key_projection, value_projection], axis=1)
    qkv_cols = qkv_shard.shape[1]
    small_row = jnp.pad(small[None, :], ((0, SMALL_ROWS - 1), (0, qkv_cols - small.shape[0])))
    pad_rows = -shard_rows % 16
    attn_shard = jnp.concatenate(
        [jnp.pad(qkv_shard, ((0, pad_rows), (0, 0))), small_row], axis=0
    )
    attn_full_shards = gather_fsdp(attn_shard)
    w_qkv = attn_full_shards[:, :shard_rows].reshape(width, qkv_cols)
    small_full = attn_full_shards[:, shard_rows + pad_rows]
    gain_one = small_full[:, :shard_rows].reshape(-1)
    gain_two = small_full[:, shard_rows : 2 * shard_rows].reshape(-1)
    at = 2 * shard_rows
    b_query = (
        small_full[:, at : at + head_count * bias_cols]
        .reshape(shards, head_count, bias_cols)
        .transpose(1, 0, 2)
        .reshape(-1)
    )
    at += head_count * bias_cols
    b_key = small_full[:, at : at + bias_cols].reshape(-1)
    b_value = small_full[:, at + bias_cols : at + 2 * bias_cols].reshape(-1)
    b_qkv = jnp.concatenate([b_query, b_key, b_value])

    o_trans = gather_fsdp(o_weight.T).reshape(width, q_cols)

    def my_columns(weight):
        return pick(
            [weight[:, i * hidden_cols : (i + 1) * hidden_cols] for i in range(ctx_count)], ctx
        )

    w_gate = gather_fsdp(my_columns(gate_weight)).reshape(width, hidden_cols)
    w_up = gather_fsdp(my_columns(up_weight)).reshape(width, hidden_cols)
    down_trans = gather_fsdp(my_columns(down_weight.T)).reshape(width, hidden_cols)

    grad_low = out_grad[0]
    grad_others = ctx_blocks(grad_low)

    first_row = ctx * row_count
    inputs = wide(tokens[0])
    seq_positions = positions[0]
    token_index = first_row + jnp.arange(row_count, dtype=jnp.int32)
    doc_start = token_index - seq_positions
    token_rows = jnp.stack([token_index, doc_start])
    bases = jnp.stack([lax.rem(ctx + ahead, ctx_count) * row_count for ahead in range(1, ctx_count + 1)])
    inv_freq = 1000000.0 ** (-jnp.arange(0, head_dim, 2, dtype=jnp.float32) / head_dim)
    angles = inv_freq[:, None] * wide(seq_positions)[None, :]
    angles = jnp.concatenate([angles, angles], axis=0)
    cosine = jnp.cos(angles)
    sine = jnp.sin(angles)
    inv_one = lax.rsqrt(jnp.mean(inputs * inputs, axis=-1, keepdims=True) + NORM_EPS)
    first_norm = low(inputs * inv_one * wide(gain_one))
    qkv_lin = lax.dot_general(
        w_qkv, first_norm, (((0,), (1,)), ((), ())), preferred_element_type=jnp.float32
    ) + wide(b_qkv)[:, None]
    heads_lin = qkv_lin[: q_cols + head_dim].reshape(head_count + 1, head_dim, row_count)
    rotated = low(heads_lin * cosine + turn_halves(heads_lin) * sine)
    queries = (rotated[:head_count] * jnp.bfloat16(score_scale)).reshape(q_cols, row_count)
    key_value = jnp.concatenate([rotated[head_count], low(qkv_lin[q_cols + head_dim :])], axis=0)
    kv_all = jnp.concatenate(
        [from_ctx(key_value, ahead) for ahead in range(1, ctx_count)] + [key_value], axis=1
    )
    keys_t, values_t = kv_all[:head_dim], kv_all[head_dim:]
    keys, values = keys_t.T, values_t.T
    attn_full, attn_low, logs = attend(bases, token_rows, queries, keys, values_t, head_count)
    out_part = low(
        lax.dot_general(
            attn_low, o_trans, (((0,), (1,)), ((), ())), preferred_element_type=jnp.float32
        )
    )
    middle = inputs + (wide(out_part) + wide(swap_cores(out_part)))
    inv_two = lax.rsqrt(jnp.mean(middle * middle, axis=-1, keepdims=True) + NORM_EPS)
    norm_two = low(middle * inv_two * wide(gain_two))
    norm_blocks = [norm_two] + ctx_blocks(norm_two)
    grad_blocks = [grad_low] + grad_others

    hidden_blocks, gate_grads, up_grads, norm_parts, down_parts = [], [], [], [], []
    for norm_block, grad_block in zip(norm_blocks, grad_blocks):
        hidden_grad = product(grad_block, down_trans)
        gate_proj = product(norm_block, w_gate)
        up_proj = product(norm_block, w_up)
        sigmoid_gate = jax.nn.sigmoid(gate_proj)
        silu_gate = gate_proj * sigmoid_gate
        hidden_blocks.append(low(silu_gate * up_proj))
        gate_grads.append(
            low(hidden_grad * up_proj * sigmoid_gate * (1.0 + gate_proj * (1.0 - sigmoid_gate)))
        )
        up_grads.append(low(hidden_grad * silu_gate))
        norm_parts.append(
            low(times_trans(gate_grads[-1], w_gate) + times_trans(up_grads[-1], w_up))
        )
        down_parts.append(low(times_trans(hidden_blocks[-1], down_trans)))
    norm_two_grad = wide(block_sums(norm_parts[0], norm_parts[1:]))
    layer_out = low(middle + wide(block_sums(down_parts[0], down_parts[1:])))
    norm_all = jnp.concatenate([block.T for block in norm_blocks], axis=1)
    grad_all = jnp.concatenate([block.T for block in grad_blocks], axis=1)

    def ff_share(left, right_blocks):
        right = jnp.concatenate(right_blocks, axis=0)
        low_share = low(scatter_sum(*weight_grad(own_x, left, right, False, shards)))
        parts = [low_share] + [from_ctx(low_share, ahead) for ahead in range(1, ctx_count)]
        return jnp.concatenate(
            [wide(pick(parts, lax.rem(i - ctx + ctx_count, ctx_count))) for i in range(ctx_count)],
            axis=1,
        )

    down_share = ff_share(grad_all, hidden_blocks).T
    gate_share = ff_share(norm_all, gate_grads)
    up_share = ff_share(norm_all, up_grads)

    grad_top = wide(grad_low)
    middle_part, gain_two_grad = norm_back(norm_two_grad, middle, inv_two, wide(gain_two))
    middle_grad = grad_top + middle_part
    middle_low = low(middle_grad)
    attn_grad = low(
        lax.dot_general(
            o_trans, middle_low, (((0,), (1,)), ((), ())), preferred_element_type=jnp.float32
        )
    )
    query_grad, pair_grad = attend_back(
        bases, token_rows, queries, keys, values, keys_t, attn_grad, attn_full, logs, cosine, sine,
        head_count, score_scale,
    )
    pair_mine = wide(pair_grad[:, (ctx_count - 1) * row_count :])
    for ahead in range(1, ctx_count):
        pair_mine = pair_mine + wide(
            to_ctx(pair_grad[:, (ahead - 1) * row_count : ahead * row_count], ahead)
        )
    key_grad = low(unrotate(pair_mine[:head_dim], cosine, sine))
    value_grad = low(pair_mine[head_dim:])
    qkv_grad = jnp.concatenate([query_grad, key_grad, value_grad], axis=0)
    bias_grad = low(jnp.sum(wide(qkv_grad), axis=1))
    norm_one_part = low(
        lax.dot_general(
            qkv_grad, w_qkv, (((0,), (1,)), ((), ())), preferred_element_type=jnp.float32
        )
    )
    norm_one_grad = wide(norm_one_part) + wide(swap_cores(norm_one_part))
    input_part, gain_one_grad = norm_back(norm_one_grad, inputs, inv_one, wide(gain_one))
    input_grad = middle_grad + input_part

    small_grad = jnp.concatenate(
        [
            low(gain_one_grad).reshape(shards, shard_rows),
            low(gain_two_grad).reshape(shards, shard_rows),
            bias_grad[:q_cols]
            .reshape(head_count, shards, bias_cols)
            .transpose(1, 0, 2)
            .reshape(shards, head_count * bias_cols),
            bias_grad[q_cols : q_cols + head_dim].reshape(shards, bias_cols),
            bias_grad[q_cols + head_dim :].reshape(shards, bias_cols),
        ],
        axis=1,
    )
    small_grad = jnp.pad(
        small_grad[:, None, :],
        ((0, 0), (pad_rows, SMALL_ROWS - 1), (0, qkv_cols - small_grad.shape[1])),
    )

    def ctx_sum(value):
        value = low(value)
        total = wide(value)
        for ahead in range(1, ctx_count):
            total = total + wide(from_ctx(value, ahead))
        return total

    o_share = ctx_sum(
        scatter_sum(*weight_grad(own_x, middle_low.T, attn_low, True, shards))
    ).T
    attn_share = ctx_sum(
        scatter_sum(*weight_grad(own_x, first_norm.T, qkv_grad, True, shards, small_grad))
    )
    small_share = attn_share[shard_rows + pad_rows]
    at = 2 * shard_rows
    q_bias_end = at + head_count * bias_cols
    return (
        layer_out[None],
        input_grad[None],
        small_share[:shard_rows],
        attn_share[:shard_rows, :q_cols],
        small_share[at:q_bias_end].reshape(head_count, bias_cols),
        attn_share[:shard_rows, q_cols : q_cols + head_dim],
        small_share[q_bias_end : q_bias_end + bias_cols][None],
        attn_share[:shard_rows, q_cols + head_dim :],
        small_share[q_bias_end + bias_cols : q_bias_end + 2 * bias_cols][None],
        o_share,
        small_share[shard_rows : 2 * shard_rows],
        gate_share,
        up_share,
        down_share,
    )


def solution(mesh):
    placed = (
        P("fsdp", "ctx", None),
        P("fsdp", "ctx"),
        P("fsdp"),
        P("fsdp", "tp"),
        P("tp", "fsdp"),
        P("fsdp", "tp"),
        P("tp", "fsdp"),
        P("fsdp", "tp"),
        P("tp", "fsdp"),
        P("tp", "fsdp"),
        P("fsdp"),
        P("fsdp", "tp"),
        P("fsdp", "tp"),
        P("tp", "fsdp"),
        P("fsdp", "ctx", None),
    )
    return jax.shard_map(
        body,
        mesh=mesh,
        in_specs=placed,
        out_specs=(
            P("fsdp", "ctx", None),
            P("fsdp", "ctx", None),
            P("fsdp"),
            P("fsdp", "tp"),
            P("tp", "fsdp"),
            P("fsdp", "tp"),
            P("tp", "fsdp"),
            P("fsdp", "tp"),
            P("tp", "fsdp"),
            P("tp", "fsdp"),
            P("fsdp"),
            P("fsdp", "tp"),
            P("fsdp", "tp"),
            P("tp", "fsdp"),
        ),
        check_vma=False,
    )
```

```python
import functools

import jax
import jax.numpy as jnp
from jax import lax
from jax.experimental import pallas as pl
from jax.experimental.pallas import tpu as pltpu
from jax.sharding import PartitionSpec as P

NORM_EPS = 1e-06
MASK_FILL = -1e30
SMALL_ROWS = 16
VMEM_BYTES = 48 * 1024 * 1024


def product(left, right):
    return jnp.dot(left, right, preferred_element_type=jnp.float32)


def inner_prod(left, right):
    return lax.dot_general(
        left, right, (((0,), (0,)), ((), ())), preferred_element_type=jnp.float32
    )


def times_trans(left, right):
    return lax.dot_general(
        left, right, (((1,), (1,)), ((), ())), preferred_element_type=jnp.float32
    )


def low(value):
    return value.astype(jnp.bfloat16)


def wide(value):
    return value.astype(jnp.float32)


def turn_halves(stack):
    half = stack.shape[1] // 2
    return jnp.concatenate([-stack[:, half:], stack[:, :half]], axis=1)


def unrotate(upstream, cosine, sine):
    half = upstream.shape[0] // 2
    shifted = upstream * sine
    turned_back = jnp.concatenate([shifted[half:], -shifted[:half]], axis=0)
    return upstream * cosine + turned_back


def fill_bias(base_ref, token_ref, bias_ref, blocks, rows, columns, span):
    token = token_ref[0:1, columns]
    begin = token_ref[1:2, columns]
    for number in range(blocks):
        size = min(rows, span - number * rows)
        index = base_ref[number] + lax.broadcasted_iota(jnp.int32, (size, token.shape[1]), 0)
        bias_ref[number * rows : number * rows + size, :] = jnp.where(
            (index <= token) & (index >= begin), 0.0, MASK_FILL
        )


def attend_kernel(heads, size, blocks, base_ref, token_ref, q_ref, k_ref, v_ref, *refs):
    attn_ref, low_ref, log_ref, bias_ref = refs[-4:]
    rows = q_ref.shape[1]
    tile = bias_ref.shape[1]
    for start in range(0, rows, tile):
        columns = slice(start, start + tile)
        span = (blocks - 1) * rows + start + tile
        fill_bias(base_ref, token_ref, bias_ref, blocks, rows, columns, span)
        for head in range(heads):
            at = slice(head * size, (head + 1) * size)
            scores = product(k_ref[:span, :], q_ref[at, columns]) + bias_ref[:span, :]
            top = jnp.max(scores, axis=0, keepdims=True)
            weights = jnp.exp(scores - top)
            total = jnp.sum(weights, axis=0, keepdims=True)
            attn = product(v_ref[:, :span], low(weights)) / total
            attn_ref[at, columns] = attn
            low_ref[at, columns] = low(attn)
            log_ref[head : head + 1, columns] = top + jnp.log(total)


def attend_back_kernel(
    heads, size, blocks, scale, base_ref, token_ref, q_ref, k_ref, v_ref, kt_ref, grad_ref, attn_ref, log_ref,
    cosine_ref, sine_ref, query_grad_ref, pair_ref, bias_ref, dk_ref, dv_ref,
):
    rows = q_ref.shape[1]
    tile = bias_ref.shape[1]
    dk_ref[...] = jnp.zeros_like(dk_ref)
    dv_ref[...] = jnp.zeros_like(dv_ref)
    for start in range(0, rows, tile):
        columns = slice(start, start + tile)
        span = (blocks - 1) * rows + start + tile
        fill_bias(base_ref, token_ref, bias_ref, blocks, rows, columns, span)
        for head in range(heads):
            at = slice(head * size, (head + 1) * size)
            query = q_ref[at, columns]
            grad = grad_ref[at, columns]
            scores = product(k_ref[:span, :], query) + bias_ref[:span, :]
            probs = jnp.exp(scores - log_ref[head : head + 1, columns])
            delta = jnp.sum(wide(grad) * attn_ref[at, columns], axis=0, keepdims=True)
            score_grad = low(probs * (product(v_ref[:span, :], grad) - delta))
            dk_ref[:span, :] += times_trans(score_grad, query)
            dv_ref[:span, :] += times_trans(low(probs), grad)
            query_grad = product(kt_ref[:, :span], score_grad) * scale
            query_grad_ref[at, columns] = low(
                unrotate(query_grad, cosine_ref[:, columns], sine_ref[:, columns])
            )
    pair_ref[:size, :] = low(dk_ref[...].T)
    pair_ref[size:, :] = low(dv_ref[...].T)


QUICK = pl.CostEstimate(flops=1, bytes_accessed=1, transcendentals=0)


def kernel_params():
    return pltpu.CompilerParams(vmem_limit_bytes=VMEM_BYTES)


def in_vmem(count):
    return [pl.BlockSpec(memory_space=pltpu.VMEM)] * count


def attend(bases, token_rows, queries, keys, values_t, heads, earlier):
    width, rows = queries.shape
    tile = min(256, rows)
    return pl.pallas_call(
        functools.partial(attend_kernel, heads, width // heads, bases.shape[0]),
        out_shape=(
            jax.ShapeDtypeStruct((width, rows), jnp.float32),
            jax.ShapeDtypeStruct((width, rows), jnp.bfloat16),
            jax.ShapeDtypeStruct((heads, rows), jnp.float32),
        ),
        in_specs=[pl.BlockSpec(memory_space=pltpu.SMEM)]
        + in_vmem(4)
        + [pl.BlockSpec(memory_space=pl.ANY)] * len(earlier),
        out_specs=tuple(in_vmem(3)),
        scratch_shapes=[pltpu.VMEM((keys.shape[0], tile), jnp.float32)],
        compiler_params=kernel_params(),
        cost_estimate=QUICK,
    )(bases, token_rows, queries, keys, values_t, *earlier)


def attend_back(bases, token_rows, queries, keys, values, keys_t, grads, attn, logs, cosine, sine, heads, scale):
    width, rows = queries.shape
    size = width // heads
    total = keys.shape[0]
    tile = min(256, rows)
    return pl.pallas_call(
        functools.partial(attend_back_kernel, heads, size, bases.shape[0], scale),
        out_shape=(
            jax.ShapeDtypeStruct((width, rows), jnp.bfloat16),
            jax.ShapeDtypeStruct((2 * size, total), jnp.bfloat16),
        ),
        in_specs=[pl.BlockSpec(memory_space=pltpu.SMEM)] + in_vmem(10),
        out_specs=tuple(in_vmem(2)),
        scratch_shapes=[
            pltpu.VMEM((total, tile), jnp.float32),
            pltpu.VMEM((total, size), jnp.float32),
            pltpu.VMEM((total, size), jnp.float32),
        ],
        compiler_params=kernel_params(),
        cost_estimate=QUICK,
    )(bases, token_rows, queries, keys, values, keys_t, grads, attn, logs, cosine, sine)


def weight_grad_kernel(right_trans, order, left_ref, right_ref, *refs):
    kept_ref, sent_ref = refs[-2:]
    multiply = times_trans if right_trans else product
    full = multiply(left_ref[...], right_ref[...])
    rows = full.shape[0] // len(order)
    half = len(order) // 2
    for number, slot in enumerate(order):
        out_ref = kept_ref if number < half else sent_ref
        at = number % half * rows
        out_ref[at : at + rows, :] = low(full[slot * rows : (slot + 1) * rows])


def attn_grad_kernel(o_at, qkv_left_ref, qkv_right_ref, o_left_ref, o_right_ref, kept_ref, sent_ref):
    qkv = low(times_trans(qkv_left_ref[...], qkv_right_ref[...]))
    out = low(times_trans(o_left_ref[...], o_right_ref[...]))
    half = qkv.shape[0] // 2
    for out_ref, rows in ((kept_ref, slice(0, half)), (sent_ref, slice(half, None))):
        if qkv.shape[1] < o_at:
            out_ref[:, qkv.shape[1] : o_at] = jnp.zeros((half, o_at - qkv.shape[1]), jnp.bfloat16)
        out_ref[:, : qkv.shape[1]] = qkv[rows]
        out_ref[:, o_at:] = out[rows]


def attn_weight_grad(qkv_left, qkv_right, o_left, o_right):
    o_at = (qkv_right.shape[0] + 127) // 128 * 128
    half = jax.ShapeDtypeStruct(
        (qkv_left.shape[0] // 2, o_at + o_right.shape[0]), jnp.bfloat16
    )
    kept, sent = pl.pallas_call(
        functools.partial(attn_grad_kernel, o_at),
        out_shape=(half, half),
        in_specs=in_vmem(4),
        out_specs=tuple(in_vmem(2)),
        compiler_params=kernel_params(),
        cost_estimate=QUICK,
    )(qkv_left, qkv_right, o_left, o_right)
    return [kept, flip(sent, 0)], o_at


def slot_order(first_bits):
    bits = index_bits()
    order = []
    for number in range(1 << bits):
        slot = 0
        for place, bit in enumerate(first_bits):
            slot |= ((number >> (bits - 1 - place)) & 1) << (bits - 1 - bit)
        order.append(slot)
    return order


def weight_grad(left, right, right_trans, bits, earlier=()):
    cols = right.shape[0] if right_trans else right.shape[1]
    half = jax.ShapeDtypeStruct((left.shape[0] // 2, cols), jnp.bfloat16)
    kept, sent = pl.pallas_call(
        functools.partial(weight_grad_kernel, right_trans, slot_order(bits)),
        out_shape=(half, half),
        in_specs=in_vmem(2) + [pl.BlockSpec(memory_space=pl.ANY)] * len(earlier),
        out_specs=tuple(in_vmem(2)),
        compiler_params=kernel_params(),
        cost_estimate=QUICK,
    )(left, right, *earlier)
    return [kept, flip(sent, bits[0])]


def norm_back(upstream, source, inverse, gain_vec):
    scaled = upstream * gain_vec
    gain_grad = jnp.sum(upstream * source * inverse, axis=0)
    input_part = inverse * scaled - source * inverse**3 * jnp.mean(
        scaled * source, axis=-1, keepdims=True
    )
    return (input_part, gain_grad)


def index_bits():
    return (lax.axis_size("fsdp") - 1).bit_length()


def flip(value, bit):
    count = lax.axis_size("fsdp")
    return lax.ppermute(value, "fsdp", [(i, i ^ (1 << bit)) for i in range(count)])


def own_bit(bit):
    return lax.rem(lax.axis_index("fsdp") // (1 << bit), 2)


def after(value, *earlier):
    for other in earlier:
        first = other[(0,) * other.ndim]
        value = value + jnp.minimum(jnp.abs(first), 0).astype(value.dtype)
    return value


def slot_chunks():
    bits = index_bits()
    reversed_bits = [
        sum(((slot >> bit) & 1) << (bits - 1 - bit) for bit in range(bits))
        for slot in range(1 << bits)
    ]
    return jnp.array(reversed_bits, jnp.int32) ^ lax.axis_index("fsdp")


def scatter_step(parts, bit, *earlier):
    half = parts[0].shape[0] // 2

    def cut(start):
        return after(low(sum(wide(part[start : start + half]) for part in parts)), *earlier)

    return [cut(0), flip(cut(half), bit)]


def scatter_rest_parts(parts, bits, *earlier):
    for number, bit in enumerate(bits):
        parts = scatter_step(parts, bit, *(earlier if number == 0 else ()))
    return parts


def scatter_rest(parts, bits, *earlier):
    parts = scatter_rest_parts(parts, bits, *earlier)
    return wide(parts[0]) + wide(parts[1])


def swap_cores(value):
    count = lax.axis_size("tp")
    return lax.ppermute(value, "tp", [(i, (i + 1) % count) for i in range(count)])


def from_ctx(value, ahead):
    count = lax.axis_size("ctx")
    return lax.ppermute(value, "ctx", [((i + ahead) % count, i) for i in range(count)])


def to_ctx(value, ahead):
    count = lax.axis_size("ctx")
    return lax.ppermute(value, "ctx", [(i, (i + ahead) % count) for i in range(count)])


def ctx_blocks(value):
    return [from_ctx(value, ahead) for ahead in range(1, lax.axis_size("ctx"))]


def add_blocks(own, received):
    total = wide(own)
    for part in received:
        total = total + wide(part)
    total = low(total)
    return low(wide(total) + wide(swap_cores(total)))


def send_blocks(others):
    return [to_ctx(other, ahead + 1) for ahead, other in enumerate(others)]


def pick(choices, index):
    out = choices[0]
    for number, choice in enumerate(choices[1:], 1):
        out = jnp.where(index == number, choice, out)
    return out


def body(
    tokens,
    positions,
    norm1_gain,
    q_weight,
    q_bias,
    key_projection,
    key_bias,
    value_projection,
    value_bias,
    o_weight,
    norm2_gain,
    gate_weight,
    up_weight,
    down_weight,
    out_grad,
):
    row_count, width = tokens.shape[1:]
    shards = lax.axis_size("fsdp")
    ctx_count = lax.axis_size("ctx")
    ctx = lax.axis_index("ctx")
    head_dim = key_projection.shape[1]
    head_count = q_weight.shape[1] // head_dim
    q_cols = head_count * head_dim
    score_scale = head_dim ** (-0.5)
    shard_rows = q_weight.shape[0]
    chunks = slot_chunks()
    column = jnp.arange(width, dtype=jnp.int32)
    place = jnp.repeat(chunks * shard_rows, shard_rows) + column % shard_rows
    to_slots = (column[:, None] == place[None, :]).astype(jnp.bfloat16)
    slot_of = (jnp.arange(shards, dtype=jnp.int32)[:, None] == chunks[None, :]).astype(jnp.float32)
    hidden_cols = gate_weight.shape[1] // ctx_count
    bias_cols = q_bias.shape[1]

    small = jnp.concatenate(
        [norm1_gain, norm2_gain, q_bias.reshape(-1), key_bias.reshape(-1), value_bias.reshape(-1)]
    )
    qkv_shard = jnp.concatenate([q_weight, key_projection, value_projection], axis=1)
    qkv_cols = qkv_shard.shape[1]
    small_row = jnp.pad(small[None, :], ((0, SMALL_ROWS - 1), (0, qkv_cols - small.shape[0])))
    pad_rows = -shard_rows % 16
    attn_shard = jnp.concatenate(
        [jnp.pad(qkv_shard, ((0, pad_rows), (0, 0))), small_row], axis=0
    )

    def my_columns(weight):
        return pick(
            [weight[:, i * hidden_cols : (i + 1) * hidden_cols] for i in range(ctx_count)], ctx
        )

    got = {}

    def stages(name, full, bits, *earlier):
        for bit in bits:
            full = after(full, *earlier)
            earlier = ()
            got[name, bit] = flip(full, bit)
            full = jnp.concatenate([full, got[name, bit]], axis=0)
        return full

    top = index_bits() - 1
    high = list(range(top, 0, -1))
    down_order = range(shards)
    down_full = stages("down", my_columns(down_weight.T)[None], [0])
    attn_full = stages("attn", attn_shard[None], high)
    gate_full = stages("gate", my_columns(gate_weight)[None], high)
    attn_full_shards = stages("attn", attn_full, [0])
    grad_low = low(product(out_grad[0], to_slots))
    grad_others = ctx_blocks(grad_low)
    o_full = stages("o", o_weight.T[None], high + [0], got["attn", top])
    gate_full = stages("gate", gate_full, [0])
    up_full = stages("up", my_columns(up_weight)[None], high + [0], got["attn", 1])
    for bit in high:
        earlier = (got["up", top], got["o", top]) if bit == top else ()
        down_full = stages("down", down_full, [bit], *earlier)
    half = shards // 2
    down_full = jnp.concatenate(
        [down_full[2 * (slot % half) + slot // half][None] for slot in down_order], axis=0
    )
    w_qkv = attn_full_shards[:, :shard_rows].reshape(width, qkv_cols)
    small_full = attn_full_shards[:, shard_rows + pad_rows]
    bias_rows = low(product(slot_of, wide(small_full[:, 2 * shard_rows :])))
    gain_one = small_full[:, :shard_rows].reshape(-1)
    gain_two = small_full[:, shard_rows : 2 * shard_rows].reshape(-1)
    at = head_count * bias_cols
    b_query = (
        bias_rows[:, :at].reshape(shards, head_count, bias_cols).transpose(1, 0, 2).reshape(-1)
    )
    b_key = bias_rows[:, at : at + bias_cols].reshape(-1)
    b_value = bias_rows[:, at + bias_cols : at + 2 * bias_cols].reshape(-1)
    b_qkv = jnp.concatenate([b_query, b_key, b_value])

    o_trans = o_full.reshape(width, q_cols)
    w_gate = gate_full.reshape(width, hidden_cols)
    w_up = up_full.reshape(width, hidden_cols)
    down_trans = down_full.reshape(width, hidden_cols)

    first_row = ctx * row_count
    inputs = product(tokens[0], to_slots)
    seq_positions = positions[0]
    token_index = first_row + jnp.arange(row_count, dtype=jnp.int32)
    doc_start = token_index - seq_positions
    token_rows = jnp.stack([token_index, doc_start])
    bases = jnp.stack([lax.rem(ctx + ahead, ctx_count) * row_count for ahead in range(1, ctx_count + 1)])
    inv_freq = 1000000.0 ** (-jnp.arange(0, head_dim, 2, dtype=jnp.float32) / head_dim)
    angles = inv_freq[:, None] * wide(seq_positions)[None, :]
    angles = jnp.concatenate([angles, angles], axis=0)
    cosine = jnp.cos(angles)
    sine = jnp.sin(angles)
    inv_one = lax.rsqrt(jnp.mean(inputs * inputs, axis=-1, keepdims=True) + NORM_EPS)
    first_norm = low(inputs * inv_one * wide(gain_one))
    qkv_lin = lax.dot_general(
        w_qkv, first_norm, (((0,), (1,)), ((), ())), preferred_element_type=jnp.float32
    ) + wide(b_qkv)[:, None]
    heads_lin = qkv_lin[: q_cols + head_dim].reshape(head_count + 1, head_dim, row_count)
    rotated = low(heads_lin * cosine + turn_halves(heads_lin) * sine)
    queries = (rotated[:head_count] * jnp.bfloat16(score_scale)).reshape(q_cols, row_count)
    key_value = jnp.concatenate([rotated[head_count], low(qkv_lin[q_cols + head_dim :])], axis=0)
    kv_all = jnp.concatenate(
        [from_ctx(key_value, ahead) for ahead in range(1, ctx_count)] + [key_value], axis=1
    )
    keys_t, values_t = kv_all[:head_dim], kv_all[head_dim:]
    keys, values = keys_t.T, values_t.T
    attn_full, attn_low, logs = attend(
        bases, token_rows, queries, keys, values_t, head_count, ()
    )
    out_part = low(
        lax.dot_general(
            attn_low, o_trans, (((0,), (1,)), ((), ())), preferred_element_type=jnp.float32
        )
    )
    middle = inputs + (wide(out_part) + wide(swap_cores(out_part)))
    inv_two = lax.rsqrt(jnp.mean(middle * middle, axis=-1, keepdims=True) + NORM_EPS)
    norm_two = low(middle * inv_two * wide(gain_two))
    norm_blocks = [norm_two] + ctx_blocks(norm_two)
    grad_blocks = [grad_low] + grad_others

    hidden_blocks, gate_grads, up_grads, norm_parts, down_parts = [], [], [], [], []
    for norm_block, grad_block in zip(norm_blocks, grad_blocks):
        hidden_grad = product(grad_block, down_trans)
        gate_proj = product(norm_block, w_gate)
        up_proj = product(norm_block, w_up)
        sigmoid_gate = jax.nn.sigmoid(gate_proj)
        silu_gate = gate_proj * sigmoid_gate
        hidden_blocks.append(low(silu_gate * up_proj))
        gate_grads.append(
            low(hidden_grad * up_proj * sigmoid_gate * (1.0 + gate_proj * (1.0 - sigmoid_gate)))
        )
        up_grads.append(low(hidden_grad * silu_gate))
        norm_parts.append(
            low(times_trans(gate_grads[-1], w_gate) + times_trans(up_grads[-1], w_up))
        )
        down_parts.append(low(times_trans(hidden_blocks[-1], down_trans)))
    norm_received = send_blocks(norm_parts[1:])
    norm_all = jnp.concatenate([block.T for block in norm_blocks], axis=1)
    grad_all = jnp.concatenate([block.T for block in grad_blocks], axis=1)

    low_first = list(range(index_bits()))
    x_last = low_first[1:] + [0]

    def ff_start(left, right_blocks, bits, *earlier):
        return weight_grad(
            left, jnp.concatenate(right_blocks, axis=0), False, bits, earlier=earlier
        )

    def ff_end(run, *earlier):
        low_share = after(low(wide(run[0]) + wide(run[1])), *earlier)
        parts = [low_share] + [from_ctx(low_share, ahead) for ahead in range(1, ctx_count)]
        return low_share, jnp.concatenate(
            [wide(pick(parts, lax.rem(i - ctx + ctx_count, ctx_count))) for i in range(ctx_count)],
            axis=1,
        )

    down_run = ff_start(grad_all, hidden_blocks, low_first)
    up_run = ff_start(norm_all, up_grads, x_last, down_run[0])
    gate_run = ff_start(norm_all, gate_grads, low_first, up_run[0])

    norm_two_grad = wide(
        add_blocks(after(norm_parts[0], gate_run[0]), norm_received)
    )
    down_received = send_blocks([after(part, norm_two_grad) for part in down_parts[1:]])
    grad_top = wide(grad_low)
    middle_part, gain_two_grad = norm_back(norm_two_grad, middle, inv_two, wide(gain_two))
    middle_grad = grad_top + middle_part
    middle_low = low(middle_grad)
    attn_grad = low(
        lax.dot_general(
            o_trans, middle_low, (((0,), (1,)), ((), ())), preferred_element_type=jnp.float32
        )
    )
    query_grad, pair_grad = attend_back(
        bases, token_rows, queries, keys, values, keys_t, attn_grad, attn_full, logs, cosine, sine,
        head_count, score_scale,
    )
    up_run = scatter_step(up_run, x_last[1], query_grad)
    down_run = scatter_step(down_run, low_first[1], query_grad)
    pair_mine = wide(pair_grad[:, (ctx_count - 1) * row_count :])
    for ahead in range(1, ctx_count):
        pair_mine = pair_mine + wide(
            to_ctx(pair_grad[:, (ahead - 1) * row_count : ahead * row_count], ahead)
        )
    key_grad = low(unrotate(pair_mine[:head_dim], cosine, sine))
    value_grad = low(pair_mine[head_dim:])
    qkv_grad = jnp.concatenate([query_grad, key_grad, value_grad], axis=0)
    bias_grad = low(jnp.sum(wide(qkv_grad), axis=1))
    attn_run, o_at = attn_weight_grad(first_norm.T, qkv_grad, middle_low.T, attn_low)
    kept = attn_run[0]
    norm_one_part = low(
        lax.dot_general(
            qkv_grad, w_qkv, (((0,), (1,)), ((), ())), preferred_element_type=jnp.float32
        )
    )
    norm_one_grad = wide(norm_one_part) + wide(swap_cores(norm_one_part))
    input_part, gain_one_grad = norm_back(norm_one_grad, inputs, inv_one, wide(gain_one))
    input_grad = middle_grad + input_part

    bias_grad = jnp.concatenate(
        [
            bias_grad[:q_cols]
            .reshape(head_count, shards, bias_cols)
            .transpose(1, 0, 2)
            .reshape(shards, head_count * bias_cols),
            bias_grad[q_cols : q_cols + head_dim].reshape(shards, bias_cols),
            bias_grad[q_cols + head_dim :].reshape(shards, bias_cols),
        ],
        axis=1,
    )
    small_grad = jnp.concatenate(
        [
            gain_one_grad.reshape(shards, shard_rows),
            gain_two_grad.reshape(shards, shard_rows),
            inner_prod(slot_of, wide(bias_grad)),
        ],
        axis=1,
    )
    def ctx_sum(value):
        value = low(value)
        total = wide(value)
        for ahead in range(1, ctx_count):
            total = total + wide(from_ctx(value, ahead))
        return total

    gate_run = scatter_step(gate_run, low_first[1], kept)
    up_run = scatter_rest_parts(up_run, x_last[2:], kept)
    down_run = scatter_rest_parts(down_run, low_first[2:], kept)
    attn_run = scatter_step(attn_run, low_first[1], up_run[0], down_run[0])
    gate_run = scatter_rest_parts(gate_run, low_first[2:], attn_run[0])
    up_low, up_share = ff_end(up_run, gate_run[0])
    down_low, down_share = ff_end(down_run, gate_run[0])
    down_share = down_share.T
    attn_run = scatter_rest_parts(attn_run, low_first[2:], up_low, down_low)
    small_grad = jnp.pad(small_grad, ((0, 0), (0, -small_grad.shape[1] % 128)))
    small_grad = after(small_grad, gate_run[0])
    for bit in low_first:
        half = small_grad.shape[0] // 2
        small_grad = small_grad[:half] + flip(small_grad[half:], bit)
    small_share = small_grad[0]
    for ahead in range(1, ctx_count):
        small_share = small_share + from_ctx(small_grad[0], ahead)

    layer_out = low(middle + wide(add_blocks(after(down_parts[0], attn_run[0]), down_received)))
    gate_low, gate_share = ff_end(gate_run)
    attn_share = ctx_sum(wide(attn_run[0]) + wide(attn_run[1]))
    o_share = attn_share[:, o_at:].T
    at = 2 * shard_rows
    q_bias_end = at + head_count * bias_cols
    layer_out = low(times_trans(layer_out, to_slots))
    input_high = low(input_grad)
    input_rest = low(input_grad - wide(input_high))
    input_grad = times_trans(input_high, to_slots) + times_trans(input_rest, to_slots)
    return (
        layer_out[None],
        input_grad[None],
        small_share[:shard_rows],
        attn_share[:, :q_cols],
        small_share[at:q_bias_end].reshape(head_count, bias_cols),
        attn_share[:, q_cols : q_cols + head_dim],
        small_share[q_bias_end : q_bias_end + bias_cols][None],
        attn_share[:, q_cols + head_dim : qkv_cols],
        small_share[q_bias_end + bias_cols : q_bias_end + 2 * bias_cols][None],
        o_share,
        small_share[shard_rows : 2 * shard_rows],
        gate_share,
        up_share,
        down_share,
    )


def solution(mesh):
    placed = (
        P("fsdp", "ctx", None),
        P("fsdp", "ctx"),
        P("fsdp"),
        P("fsdp", "tp"),
        P("tp", "fsdp"),
        P("fsdp", "tp"),
        P("tp", "fsdp"),
        P("fsdp", "tp"),
        P("tp", "fsdp"),
        P("tp", "fsdp"),
        P("fsdp"),
        P("fsdp", "tp"),
        P("fsdp", "tp"),
        P("tp", "fsdp"),
        P("fsdp", "ctx", None),
    )
    return jax.shard_map(
        body,
        mesh=mesh,
        in_specs=placed,
        out_specs=(
            P("fsdp", "ctx", None),
            P("fsdp", "ctx", None),
            P("fsdp"),
            P("fsdp", "tp"),
            P("tp", "fsdp"),
            P("fsdp", "tp"),
            P("tp", "fsdp"),
            P("fsdp", "tp"),
            P("tp", "fsdp"),
            P("tp", "fsdp"),
            P("fsdp"),
            P("fsdp", "tp"),
            P("fsdp", "tp"),
            P("tp", "fsdp"),
        ),
        check_vma=False,
    )
```

```python
import functools

import jax
import jax.numpy as jnp
from jax import lax
from jax.experimental import pallas as pl
from jax.experimental.pallas import tpu as pltpu
from jax.sharding import PartitionSpec as P

NORM_EPS = 1e-06
MASK_FILL = -1e30
SMALL_ROWS = 16
VMEM_BYTES = 48 * 1024 * 1024


def product(left, right):
    return jnp.dot(left, right, preferred_element_type=jnp.float32)


def inner_prod(left, right):
    return lax.dot_general(
        left, right, (((0,), (0,)), ((), ())), preferred_element_type=jnp.float32
    )


def times_trans(left, right):
    return lax.dot_general(
        left, right, (((1,), (1,)), ((), ())), preferred_element_type=jnp.float32
    )


def low(value):
    return value.astype(jnp.bfloat16)


def wide(value):
    return value.astype(jnp.float32)


def turn_halves(stack):
    half = stack.shape[1] // 2
    return jnp.concatenate([-stack[:, half:], stack[:, :half]], axis=1)


def unrotate(upstream, cosine, sine):
    half = upstream.shape[0] // 2
    shifted = upstream * sine
    turned_back = jnp.concatenate([shifted[half:], -shifted[:half]], axis=0)
    return upstream * cosine + turned_back


def fill_bias(base_ref, token_ref, bias_ref, blocks, rows, columns, span):
    token = token_ref[0:1, columns]
    begin = token_ref[1:2, columns]
    for number in range(blocks):
        size = min(rows, span - number * rows)
        index = base_ref[number] + lax.broadcasted_iota(jnp.int32, (size, token.shape[1]), 0)
        bias_ref[number * rows : number * rows + size, :] = jnp.where(
            (index <= token) & (index >= begin), 0.0, MASK_FILL
        )


def attend_kernel(heads, size, blocks, base_ref, token_ref, q_ref, k_ref, v_ref, *refs):
    attn_ref, low_ref, log_ref, bias_ref = refs[-4:]
    rows = q_ref.shape[1]
    tile = bias_ref.shape[1]
    for start in range(0, rows, tile):
        columns = slice(start, start + tile)
        span = (blocks - 1) * rows + start + tile
        fill_bias(base_ref, token_ref, bias_ref, blocks, rows, columns, span)
        for head in range(heads):
            at = slice(head * size, (head + 1) * size)
            scores = product(k_ref[:span, :], q_ref[at, columns]) + bias_ref[:span, :]
            top = jnp.max(scores, axis=0, keepdims=True)
            weights = jnp.exp(scores - top)
            total = jnp.sum(weights, axis=0, keepdims=True)
            attn = product(v_ref[:, :span], low(weights)) / total
            attn_ref[at, columns] = attn
            low_ref[at, columns] = low(attn)
            log_ref[head : head + 1, columns] = top + jnp.log(total)


def attend_back_kernel(
    heads, size, blocks, scale, base_ref, token_ref, q_ref, k_ref, v_ref, kt_ref, grad_ref, attn_ref, log_ref,
    cosine_ref, sine_ref, query_grad_ref, pair_ref, bias_ref, dk_ref, dv_ref,
):
    rows = q_ref.shape[1]
    tile = bias_ref.shape[1]
    dk_ref[...] = jnp.zeros_like(dk_ref)
    dv_ref[...] = jnp.zeros_like(dv_ref)
    for start in range(0, rows, tile):
        columns = slice(start, start + tile)
        span = (blocks - 1) * rows + start + tile
        fill_bias(base_ref, token_ref, bias_ref, blocks, rows, columns, span)
        for head in range(heads):
            at = slice(head * size, (head + 1) * size)
            query = q_ref[at, columns]
            grad = grad_ref[at, columns]
            scores = product(k_ref[:span, :], query) + bias_ref[:span, :]
            probs = jnp.exp(scores - log_ref[head : head + 1, columns])
            delta = jnp.sum(wide(grad) * attn_ref[at, columns], axis=0, keepdims=True)
            score_grad = low(probs * (product(v_ref[:span, :], grad) - delta))
            dk_ref[:span, :] += times_trans(score_grad, query)
            dv_ref[:span, :] += times_trans(low(probs), grad)
            query_grad = product(kt_ref[:, :span], score_grad) * scale
            query_grad_ref[at, columns] = low(
                unrotate(query_grad, cosine_ref[:, columns], sine_ref[:, columns])
            )
    pair_ref[:size, :] = low(dk_ref[...].T)
    pair_ref[size:, :] = low(dv_ref[...].T)


QUICK = pl.CostEstimate(flops=1, bytes_accessed=1, transcendentals=0)


def kernel_params():
    return pltpu.CompilerParams(vmem_limit_bytes=VMEM_BYTES)


def in_vmem(count):
    return [pl.BlockSpec(memory_space=pltpu.VMEM)] * count


def attend(bases, token_rows, queries, keys, values_t, heads, earlier):
    width, rows = queries.shape
    tile = min(256, rows)
    return pl.pallas_call(
        functools.partial(attend_kernel, heads, width // heads, bases.shape[0]),
        out_shape=(
            jax.ShapeDtypeStruct((width, rows), jnp.float32),
            jax.ShapeDtypeStruct((width, rows), jnp.bfloat16),
            jax.ShapeDtypeStruct((heads, rows), jnp.float32),
        ),
        in_specs=[pl.BlockSpec(memory_space=pltpu.SMEM)]
        + in_vmem(4)
        + [pl.BlockSpec(memory_space=pl.ANY)] * len(earlier),
        out_specs=tuple(in_vmem(3)),
        scratch_shapes=[pltpu.VMEM((keys.shape[0], tile), jnp.float32)],
        compiler_params=kernel_params(),
        cost_estimate=QUICK,
    )(bases, token_rows, queries, keys, values_t, *earlier)


def attend_back(bases, token_rows, queries, keys, values, keys_t, grads, attn, logs, cosine, sine, heads, scale):
    width, rows = queries.shape
    size = width // heads
    total = keys.shape[0]
    tile = min(256, rows)
    return pl.pallas_call(
        functools.partial(attend_back_kernel, heads, size, bases.shape[0], scale),
        out_shape=(
            jax.ShapeDtypeStruct((width, rows), jnp.bfloat16),
            jax.ShapeDtypeStruct((2 * size, total), jnp.bfloat16),
        ),
        in_specs=[pl.BlockSpec(memory_space=pltpu.SMEM)] + in_vmem(10),
        out_specs=tuple(in_vmem(2)),
        scratch_shapes=[
            pltpu.VMEM((total, tile), jnp.float32),
            pltpu.VMEM((total, size), jnp.float32),
            pltpu.VMEM((total, size), jnp.float32),
        ],
        compiler_params=kernel_params(),
        cost_estimate=QUICK,
    )(bases, token_rows, queries, keys, values, keys_t, grads, attn, logs, cosine, sine)


def weight_grad_kernel(right_trans, order, left_ref, right_ref, *refs):
    kept_ref, sent_ref = refs[-2:]
    multiply = times_trans if right_trans else product
    full = multiply(left_ref[...], right_ref[...])
    rows = full.shape[0] // len(order)
    half = len(order) // 2
    for number, slot in enumerate(order):
        out_ref = kept_ref if number < half else sent_ref
        at = number % half * rows
        out_ref[at : at + rows, :] = low(full[slot * rows : (slot + 1) * rows])


def attn_grad_kernel(
    qkv_left_ref, qkv_right_ref, o_left_ref, o_right_ref, extra_ref, kept_ref, sent_ref
):
    qkv = times_trans(qkv_left_ref[...], qkv_right_ref[...])
    left = low(jnp.concatenate([qkv, extra_ref[...].T], axis=1))
    out = low(times_trans(o_left_ref[...], o_right_ref[...]))
    half = qkv.shape[0] // 2
    o_at = left.shape[1]
    for out_ref, rows in ((kept_ref, slice(0, half)), (sent_ref, slice(half, None))):
        out_ref[:, :o_at] = left[rows]
        out_ref[:, o_at:] = out[rows]


def attn_weight_grad(qkv_left, qkv_right, o_left, o_right, extra):
    o_at = qkv_right.shape[0] + extra.shape[0]
    half = jax.ShapeDtypeStruct(
        (qkv_left.shape[0] // 2, o_at + o_right.shape[0]), jnp.bfloat16
    )
    kept, sent = pl.pallas_call(
        attn_grad_kernel,
        out_shape=(half, half),
        in_specs=in_vmem(5),
        out_specs=tuple(in_vmem(2)),
        compiler_params=kernel_params(),
        cost_estimate=QUICK,
    )(qkv_left, qkv_right, o_left, o_right, extra)
    return [kept, flip(sent, 0)], o_at


def slot_order(first_bits):
    bits = index_bits()
    order = []
    for number in range(1 << bits):
        slot = 0
        for place, bit in enumerate(first_bits):
            slot |= ((number >> (bits - 1 - place)) & 1) << (bits - 1 - bit)
        order.append(slot)
    return order


def weight_grad(left, right, right_trans, bits, earlier=()):
    cols = right.shape[0] if right_trans else right.shape[1]
    half = jax.ShapeDtypeStruct((left.shape[0] // 2, cols), jnp.bfloat16)
    kept, sent = pl.pallas_call(
        functools.partial(weight_grad_kernel, right_trans, slot_order(bits)),
        out_shape=(half, half),
        in_specs=in_vmem(2) + [pl.BlockSpec(memory_space=pl.ANY)] * len(earlier),
        out_specs=tuple(in_vmem(2)),
        compiler_params=kernel_params(),
        cost_estimate=QUICK,
    )(left, right, *earlier)
    return [kept, flip(sent, bits[0])]


def norm_back(upstream, source, inverse, gain_vec):
    scaled = upstream * gain_vec
    gain_grad = jnp.sum(upstream * source * inverse, axis=0)
    input_part = inverse * scaled - source * inverse**3 * jnp.mean(
        scaled * source, axis=-1, keepdims=True
    )
    return (input_part, gain_grad)


def index_bits():
    return (lax.axis_size("fsdp") - 1).bit_length()


def flip(value, bit):
    count = lax.axis_size("fsdp")
    return lax.ppermute(value, "fsdp", [(i, i ^ (1 << bit)) for i in range(count)])


def own_bit(bit):
    return lax.rem(lax.axis_index("fsdp") // (1 << bit), 2)


def after(value, *earlier):
    for other in earlier:
        first = other[(0,) * other.ndim]
        value = value + jnp.minimum(jnp.abs(first), 0).astype(value.dtype)
    return value


def slot_chunks():
    bits = index_bits()
    reversed_bits = [
        sum(((slot >> bit) & 1) << (bits - 1 - bit) for bit in range(bits))
        for slot in range(1 << bits)
    ]
    return jnp.array(reversed_bits, jnp.int32) ^ lax.axis_index("fsdp")


def scatter_step(parts, bit, *earlier):
    half = parts[0].shape[0] // 2

    def cut(start):
        return after(low(sum(wide(part[start : start + half]) for part in parts)), *earlier)

    return [cut(0), flip(cut(half), bit)]


def scatter_rest_parts(parts, bits, *earlier):
    for number, bit in enumerate(bits):
        parts = scatter_step(parts, bit, *(earlier if number == 0 else ()))
    return parts


def scatter_rest(parts, bits, *earlier):
    parts = scatter_rest_parts(parts, bits, *earlier)
    return wide(parts[0]) + wide(parts[1])


def swap_cores(value):
    count = lax.axis_size("tp")
    return lax.ppermute(value, "tp", [(i, (i + 1) % count) for i in range(count)])


def from_ctx(value, ahead):
    count = lax.axis_size("ctx")
    return lax.ppermute(value, "ctx", [((i + ahead) % count, i) for i in range(count)])


def to_ctx(value, ahead):
    count = lax.axis_size("ctx")
    return lax.ppermute(value, "ctx", [(i, (i + ahead) % count) for i in range(count)])


def ctx_blocks(value):
    return [from_ctx(value, ahead) for ahead in range(1, lax.axis_size("ctx"))]


def add_blocks(own, received):
    total = wide(own)
    for part in received:
        total = total + wide(part)
    total = low(total)
    return low(wide(total) + wide(swap_cores(total)))


def send_blocks(others):
    return [to_ctx(other, ahead + 1) for ahead, other in enumerate(others)]


def pick(choices, index):
    out = choices[0]
    for number, choice in enumerate(choices[1:], 1):
        out = jnp.where(index == number, choice, out)
    return out


def body(
    tokens,
    positions,
    norm1_gain,
    q_weight,
    q_bias,
    key_projection,
    key_bias,
    value_projection,
    value_bias,
    o_weight,
    norm2_gain,
    gate_weight,
    up_weight,
    down_weight,
    out_grad,
):
    row_count, width = tokens.shape[1:]
    shards = lax.axis_size("fsdp")
    ctx_count = lax.axis_size("ctx")
    ctx = lax.axis_index("ctx")
    head_dim = key_projection.shape[1]
    head_count = q_weight.shape[1] // head_dim
    q_cols = head_count * head_dim
    score_scale = head_dim ** (-0.5)
    shard_rows = q_weight.shape[0]
    chunks = slot_chunks()
    column = jnp.arange(width, dtype=jnp.int32)
    place = jnp.repeat(chunks * shard_rows, shard_rows) + column % shard_rows
    to_slots = (column[:, None] == place[None, :]).astype(jnp.bfloat16)
    slot_of = (jnp.arange(shards, dtype=jnp.int32)[:, None] == chunks[None, :]).astype(jnp.float32)
    hidden_cols = gate_weight.shape[1] // ctx_count
    bias_cols = q_bias.shape[1]

    small = jnp.concatenate(
        [norm1_gain, norm2_gain, q_bias.reshape(-1), key_bias.reshape(-1), value_bias.reshape(-1)]
    )
    qkv_shard = jnp.concatenate([q_weight, key_projection, value_projection], axis=1)
    qkv_cols = qkv_shard.shape[1]
    small_row = jnp.pad(small[None, :], ((0, SMALL_ROWS - 1), (0, qkv_cols - small.shape[0])))
    pad_rows = -shard_rows % 16
    attn_shard = jnp.concatenate(
        [jnp.pad(qkv_shard, ((0, pad_rows), (0, 0))), small_row], axis=0
    )

    def my_columns(weight):
        return pick(
            [weight[:, i * hidden_cols : (i + 1) * hidden_cols] for i in range(ctx_count)], ctx
        )

    got = {}

    def stages(name, full, bits, *earlier):
        for bit in bits:
            full = after(full, *earlier)
            earlier = ()
            got[name, bit] = flip(full, bit)
            full = jnp.concatenate([full, got[name, bit]], axis=0)
        return full

    top = index_bits() - 1
    high = list(range(top, 0, -1))
    down_order = range(shards)
    down_full = stages("down", my_columns(down_weight.T)[None], [0])
    attn_full = stages("attn", attn_shard[None], high)
    gate_full = stages("gate", my_columns(gate_weight)[None], high)
    attn_full_shards = stages("attn", attn_full, [0])
    grad_low = low(product(out_grad[0], to_slots))
    grad_others = ctx_blocks(grad_low)
    o_full = stages("o", o_weight.T[None], high + [0], got["attn", top])
    gate_full = stages("gate", gate_full, [0])
    up_full = stages("up", my_columns(up_weight)[None], high + [0], got["attn", 1])
    for bit in high:
        earlier = (got["up", top], got["o", top]) if bit == top else ()
        down_full = stages("down", down_full, [bit], *earlier)
    half = shards // 2
    down_full = jnp.concatenate(
        [down_full[2 * (slot % half) + slot // half][None] for slot in down_order], axis=0
    )
    w_qkv = attn_full_shards[:, :shard_rows].reshape(width, qkv_cols)
    small_full = attn_full_shards[:, shard_rows + pad_rows]
    bias_rows = low(product(slot_of, wide(small_full[:, 2 * shard_rows :])))
    gain_one = small_full[:, :shard_rows].reshape(-1)
    gain_two = small_full[:, shard_rows : 2 * shard_rows].reshape(-1)
    at = head_count * bias_cols
    b_query = (
        bias_rows[:, :at].reshape(shards, head_count, bias_cols).transpose(1, 0, 2).reshape(-1)
    )
    b_key = bias_rows[:, at : at + bias_cols].reshape(-1)
    b_value = bias_rows[:, at + bias_cols : at + 2 * bias_cols].reshape(-1)
    b_qkv = jnp.concatenate([b_query, b_key, b_value])

    o_trans = o_full.reshape(width, q_cols)
    w_gate = gate_full.reshape(width, hidden_cols)
    w_up = up_full.reshape(width, hidden_cols)
    down_trans = down_full.reshape(width, hidden_cols)

    first_row = ctx * row_count
    inputs = product(tokens[0], to_slots)
    seq_positions = positions[0]
    token_index = first_row + jnp.arange(row_count, dtype=jnp.int32)
    doc_start = token_index - seq_positions
    token_rows = jnp.stack([token_index, doc_start])
    bases = jnp.stack([lax.rem(ctx + ahead, ctx_count) * row_count for ahead in range(1, ctx_count + 1)])
    inv_freq = 1000000.0 ** (-jnp.arange(0, head_dim, 2, dtype=jnp.float32) / head_dim)
    angles = inv_freq[:, None] * wide(seq_positions)[None, :]
    angles = jnp.concatenate([angles, angles], axis=0)
    cosine = jnp.cos(angles)
    sine = jnp.sin(angles)
    inv_one = lax.rsqrt(jnp.mean(inputs * inputs, axis=-1, keepdims=True) + NORM_EPS)
    first_norm = low(inputs * inv_one * wide(gain_one))
    qkv_lin = lax.dot_general(
        w_qkv, first_norm, (((0,), (1,)), ((), ())), preferred_element_type=jnp.float32
    ) + wide(b_qkv)[:, None]
    heads_lin = qkv_lin[: q_cols + head_dim].reshape(head_count + 1, head_dim, row_count)
    rotated = low(heads_lin * cosine + turn_halves(heads_lin) * sine)
    queries = (rotated[:head_count] * jnp.bfloat16(score_scale)).reshape(q_cols, row_count)
    key_value = jnp.concatenate([rotated[head_count], low(qkv_lin[q_cols + head_dim :])], axis=0)
    kv_all = jnp.concatenate(
        [from_ctx(key_value, ahead) for ahead in range(1, ctx_count)] + [key_value], axis=1
    )
    keys_t, values_t = kv_all[:head_dim], kv_all[head_dim:]
    keys, values = keys_t.T, values_t.T
    attn_full, attn_low, logs = attend(
        bases, token_rows, queries, keys, values_t, head_count, ()
    )
    out_part = low(
        lax.dot_general(
            attn_low, o_trans, (((0,), (1,)), ((), ())), preferred_element_type=jnp.float32
        )
    )
    middle = inputs + (wide(out_part) + wide(swap_cores(out_part)))
    inv_two = lax.rsqrt(jnp.mean(middle * middle, axis=-1, keepdims=True) + NORM_EPS)
    norm_two = low(middle * inv_two * wide(gain_two))
    norm_blocks = [norm_two] + ctx_blocks(norm_two)
    grad_blocks = [grad_low] + grad_others

    hidden_blocks, gate_grads, up_grads, norm_parts, down_parts = [], [], [], [], []
    for norm_block, grad_block in zip(norm_blocks, grad_blocks):
        hidden_grad = product(grad_block, down_trans)
        gate_proj = product(norm_block, w_gate)
        up_proj = product(norm_block, w_up)
        sigmoid_gate = jax.nn.sigmoid(gate_proj)
        silu_gate = gate_proj * sigmoid_gate
        hidden_blocks.append(low(silu_gate * up_proj))
        gate_grads.append(
            low(hidden_grad * up_proj * sigmoid_gate * (1.0 + gate_proj * (1.0 - sigmoid_gate)))
        )
        up_grads.append(low(hidden_grad * silu_gate))
        norm_parts.append(
            low(times_trans(gate_grads[-1], w_gate) + times_trans(up_grads[-1], w_up))
        )
        down_parts.append(low(times_trans(hidden_blocks[-1], down_trans)))
    norm_received = send_blocks(norm_parts[1:])
    norm_all = jnp.concatenate([block.T for block in norm_blocks], axis=1)
    grad_all = jnp.concatenate([block.T for block in grad_blocks], axis=1)

    low_first = list(range(index_bits()))
    x_last = low_first[1:] + [0]

    def ff_start(left, right_blocks, bits, *earlier):
        return weight_grad(
            left, jnp.concatenate(right_blocks, axis=0), False, bits, earlier=earlier
        )

    def ff_end(run, *earlier):
        low_share = after(low(wide(run[0]) + wide(run[1])), *earlier)
        parts = [low_share] + [from_ctx(low_share, ahead) for ahead in range(1, ctx_count)]
        return low_share, jnp.concatenate(
            [wide(pick(parts, lax.rem(i - ctx + ctx_count, ctx_count))) for i in range(ctx_count)],
            axis=1,
        )

    down_run = ff_start(grad_all, hidden_blocks, low_first)
    up_run = ff_start(norm_all, up_grads, x_last, down_run[0])
    gate_run = ff_start(norm_all, gate_grads, low_first, up_run[0])

    norm_two_grad = wide(
        add_blocks(after(norm_parts[0], gate_run[0]), norm_received)
    )
    down_received = send_blocks([after(part, norm_two_grad) for part in down_parts[1:]])
    grad_top = wide(grad_low)
    middle_part, gain_two_grad = norm_back(norm_two_grad, middle, inv_two, wide(gain_two))
    middle_grad = grad_top + middle_part
    middle_low = low(middle_grad)
    attn_grad = low(
        lax.dot_general(
            o_trans, middle_low, (((0,), (1,)), ((), ())), preferred_element_type=jnp.float32
        )
    )
    query_grad, pair_grad = attend_back(
        bases, token_rows, queries, keys, values, keys_t, attn_grad, attn_full, logs, cosine, sine,
        head_count, score_scale,
    )
    up_run = scatter_step(up_run, x_last[1], query_grad)
    down_run = scatter_step(down_run, low_first[1], query_grad)
    pair_mine = wide(pair_grad[:, (ctx_count - 1) * row_count :])
    for ahead in range(1, ctx_count):
        pair_mine = pair_mine + wide(
            to_ctx(pair_grad[:, (ahead - 1) * row_count : ahead * row_count], ahead)
        )
    key_grad = low(unrotate(pair_mine[:head_dim], cosine, sine))
    value_grad = low(pair_mine[head_dim:])
    qkv_grad = jnp.concatenate([query_grad, key_grad, value_grad], axis=0)
    bias_grad = low(jnp.sum(wide(qkv_grad), axis=1))
    norm_one_part = lax.dot_general(
        qkv_grad, w_qkv, (((0,), (1,)), ((), ())), preferred_element_type=jnp.float32
    )
    gain_one_grad = jnp.sum(norm_one_part * inputs * inv_one, axis=0)
    norm_one_part = low(norm_one_part)
    bias_grad = jnp.concatenate(
        [
            bias_grad[:q_cols]
            .reshape(head_count, shards, bias_cols)
            .transpose(1, 0, 2)
            .reshape(shards, head_count * bias_cols),
            bias_grad[q_cols : q_cols + head_dim].reshape(shards, bias_cols),
            bias_grad[q_cols + head_dim :].reshape(shards, bias_cols),
        ],
        axis=1,
    )
    bias_count = bias_grad.shape[1]
    bias_wide = -(-bias_count // shard_rows)
    bias_grad = jnp.pad(
        inner_prod(slot_of, wide(bias_grad)), ((0, 0), (0, bias_wide * shard_rows - bias_count))
    )
    bias_grad = bias_grad.reshape(shards, bias_wide, shard_rows).transpose(1, 0, 2)
    extra = jnp.concatenate(
        [gain_one_grad[None], gain_two_grad[None], bias_grad.reshape(bias_wide, width)], axis=0
    )
    gap = -qkv_cols % 128
    gap += 128 * (-(-max(0, extra.shape[0] - gap) // 128))
    extra = jnp.pad(extra, ((0, gap - extra.shape[0]), (0, 0)))
    attn_run, o_at = attn_weight_grad(first_norm.T, qkv_grad, middle_low.T, attn_low, extra)
    kept = attn_run[0]
    norm_one_grad = wide(norm_one_part) + wide(swap_cores(norm_one_part))
    input_part, _ = norm_back(norm_one_grad, inputs, inv_one, wide(gain_one))
    input_grad = middle_grad + input_part

    def ctx_sum(value):
        value = low(value)
        total = wide(value)
        for ahead in range(1, ctx_count):
            total = total + wide(from_ctx(value, ahead))
        return total

    gate_run = scatter_step(gate_run, low_first[1], kept)
    up_run = scatter_rest_parts(up_run, x_last[2:], kept)
    down_run = scatter_rest_parts(down_run, low_first[2:], kept)
    attn_run = scatter_step(attn_run, low_first[1], up_run[0], down_run[0])
    gate_run = scatter_rest_parts(gate_run, low_first[2:], attn_run[0])
    up_low, up_share = ff_end(up_run, gate_run[0])
    down_low, down_share = ff_end(down_run, gate_run[0])
    down_share = down_share.T
    attn_got = attn_run[1]
    attn_run = scatter_rest_parts(attn_run, low_first[2:], up_low, down_low)
    layer_out = low(middle + wide(add_blocks(after(down_parts[0], attn_run[0]), down_received)))
    gate_low, gate_share = ff_end(gate_run, attn_got)
    attn_share = ctx_sum(wide(attn_run[0]) + wide(attn_run[1]))
    o_share = attn_share[:, o_at:].T
    gain_one_share = attn_share[:, qkv_cols]
    gain_one_share = gain_one_share + swap_cores(gain_one_share)
    gain_two_share = attn_share[:, qkv_cols + 1]
    bias_share = attn_share[:, qkv_cols + 2 : qkv_cols + 2 + bias_wide].T.reshape(-1)
    q_bias_end = head_count * bias_cols
    layer_out = low(times_trans(layer_out, to_slots))
    input_high = low(input_grad)
    input_rest = low(input_grad - wide(input_high))
    input_grad = times_trans(input_high, to_slots) + times_trans(input_rest, to_slots)
    return (
        layer_out[None],
        input_grad[None],
        gain_one_share,
        attn_share[:, :q_cols],
        bias_share[:q_bias_end].reshape(head_count, bias_cols),
        attn_share[:, q_cols : q_cols + head_dim],
        bias_share[q_bias_end : q_bias_end + bias_cols][None],
        attn_share[:, q_cols + head_dim : qkv_cols],
        bias_share[q_bias_end + bias_cols : q_bias_end + 2 * bias_cols][None],
        o_share,
        gain_two_share,
        gate_share,
        up_share,
        down_share,
    )


def solution(mesh):
    placed = (
        P("fsdp", "ctx", None),
        P("fsdp", "ctx"),
        P("fsdp"),
        P("fsdp", "tp"),
        P("tp", "fsdp"),
        P("fsdp", "tp"),
        P("tp", "fsdp"),
        P("fsdp", "tp"),
        P("tp", "fsdp"),
        P("tp", "fsdp"),
        P("fsdp"),
        P("fsdp", "tp"),
        P("fsdp", "tp"),
        P("tp", "fsdp"),
        P("fsdp", "ctx", None),
    )
    return jax.shard_map(
        body,
        mesh=mesh,
        in_specs=placed,
        out_specs=(
            P("fsdp", "ctx", None),
            P("fsdp", "ctx", None),
            P("fsdp"),
            P("fsdp", "tp"),
            P("tp", "fsdp"),
            P("fsdp", "tp"),
            P("tp", "fsdp"),
            P("fsdp", "tp"),
            P("tp", "fsdp"),
            P("tp", "fsdp"),
            P("fsdp"),
            P("fsdp", "tp"),
            P("fsdp", "tp"),
            P("tp", "fsdp"),
        ),
        check_vma=False,
    )
```
